32 devices in a mesh: dp: 16 (over z, x, core), mp: 2 (over y).
Axes of the slice: x: 2, y: 2, z: 4, core: 2. Of those that a mesh axis runs over, the one named last changes fastest.
Arguments:
- tokens: bfloat16 [16384, 1152], P('dp'), may hold values from -8 to 8
- lengths: int32 [256], P('dp'), may hold values from 1 to 64, as said below
- images: bfloat16 [256, 1152], P('dp'), may hold values from -12 to 12
- pair_group: int32 [256], replicated, may hold values from 0 to 127, never falling along the last dimension, each value on 1 to 4 neighbouring positions
- w_up: bfloat16 [1152, 4304], P(None, 'mp'), may hold values from -0.1875 to 0.1875
- w_down: bfloat16 [1152, 4304], P(None, 'mp'), may hold values from -0.09375 to 0.09375
Outputs:
- caption_loss: float32 [256], P('dp')
- image_grad: float32 [256, 1152], P('dp')
- up_grad: float32 [1152, 4304], P('dp', 'mp')
- down_grad: float32 [1152, 4304], P('dp', 'mp')
The draws below stay inside these ranges and needn't reach their ends.
Inputs may be any that keep to these rules, and one draw needn't show every extreme that they name: Positions below lengths[c] of caption c are real tokens, the rest padding. `pair_group`: ids never fall along the pairs, and each id is held by 1 to 4 consecutive pairs.
All inputs are finite; a program needn't handle non-finite values.
Results may differ from the reference program's by a relative error of at most 0.0033.
Values may be sent and summed in bfloat16 or wider, within the bound.
A program may use at most 192 MiB of HBM per device.

```python
import math
import jax
import jax.numpy as jnp
import numpy as np
from jax import lax

D = 1152
FF = 4304
TOKLEN = 64
B_DEV = 16
B_TOTAL = 256


def draw_lengths(key, part):
    first, second, third = jax.random.split(jax.random.fold_in(key, 11), 3)
    raw = jax.random.randint(first, (B_TOTAL,), 1, TOKLEN + 1)
    spot_long = jax.random.randint(second, (), 0, B_TOTAL)
    offset = jax.random.randint(third, (), 1, B_TOTAL)
    spot_short = (spot_long + offset) % B_TOTAL
    raw = raw.at[spot_long].set(TOKLEN)
    raw = raw.at[spot_short].set(1)
    return raw.astype(jnp.int32)


def caption_direction(key, topic_share):
    base = jax.random.fold_in(key, 101)
    topic_key, index_key, own_key = jax.random.split(base, 3)
    topics = jax.random.normal(topic_key, (16, D), jnp.float32)
    topic_index = jax.random.randint(index_key, (B_TOTAL,), 0, 16)
    chosen = jnp.take(topics, topic_index, axis=0)
    own_part = jax.random.normal(own_key, (B_TOTAL, D), jnp.float32)
    return math.sqrt(topic_share) * chosen + math.sqrt(1.0 - topic_share) * own_part


def draw_tokens(key, part):
    noise_key = jax.random.fold_in(key, 211)
    direction = caption_direction(key, 0.18)
    noise_part = jax.random.normal(noise_key, (B_TOTAL, TOKLEN, D), jnp.float32)
    token_rows = jnp.clip(noise_part + direction[:, None, :], -8.0, 8.0)
    return token_rows.reshape(B_TOTAL * TOKLEN, D).astype(jnp.bfloat16)


def draw_images(key, part):
    noise_key = jax.random.fold_in(key, 307)
    direction = caption_direction(key, 0.18)
    noise_part = jax.random.normal(noise_key, (B_TOTAL, D), jnp.float32)
    image_rows = jnp.clip(direction + noise_part, -12.0, 12.0)
    return image_rows.astype(jnp.bfloat16)


def steps_of(stream_key, shape, cuts, smallest, high):
    def one(dim, blocks):
        heights = jax.random.uniform(jax.random.fold_in(jax.random.fold_in(stream_key, 6), dim), (blocks,), jnp.float32, smallest / len(cuts), high / len(cuts))
        return jnp.repeat(jnp.exp(heights), shape[dim] // blocks).reshape((-1,) + (1,) * (len(shape) - dim - 1))

    factor_of = one(*cuts[0])
    for cut in cuts[1:]:
        factor_of = factor_of * one(*cut)
    return factor_of


def split_up(amount, total, bound, skew):
    loads = [(1 << 20) // math.isqrt(standing ** skew) + 1 for standing in range(2, amount + 1)]
    rest, given = total - bound - (amount - 1), [1] * (amount - 1)
    while rest > 0:
        candidates = [i for i in range(amount - 1) if given[i] < bound]
        whole, remaining = sum([loads[i] for i in candidates]), rest
        for i in candidates:
            addition = min(bound - given[i], max(1, remaining * loads[i] // whole), rest)
            given[i] = given[i] + addition
            rest = rest - addition
    return np.array([bound] + given)


def uneven(key, number_of, total, limit, skew):
    if number_of == 2:
        one = jax.random.randint(key, (), max(1, total - limit), min(limit, total - 1) + 1)
        return jnp.stack([one, total - one])
    sizes = jnp.asarray(split_up(number_of, total, limit, skew), jnp.int32)
    twos = (number_of - 1) // 2
    giver, receiver = sizes[1:1 + 2 * twos:2], sizes[2:2 + 2 * twos:2]
    margin = jnp.minimum(giver - 1, limit - receiver)
    shifted = jax.random.randint(jax.random.fold_in(key, 1), (twos,), 0, 1 << 20) % (margin + 1)
    sizes = sizes.at[1:1 + 2 * twos:2].set(giver - shifted).at[2:2 + 2 * twos:2].set(receiver + shifted)
    return sizes[jax.random.permutation(jax.random.fold_in(key, 2), number_of)]


def centred(key, shape, scale, bound, cuts=(), kind=jnp.bfloat16):
    level = steps_of(key, shape, cuts, -0.22, 0.18) if cuts else 1.0
    array = jax.random.normal(key, shape, jnp.float32) * scale * level
    return jnp.minimum(jnp.maximum(array, -bound), bound).astype(kind)


def setup_inputs(seed: int = 0) -> dict:
    splits = jax.random.split(jax.random.key(seed), 7)
    tokens = draw_tokens(jax.random.fold_in(splits[6], 71), 0)
    lengths = draw_lengths(jax.random.fold_in(splits[6], 71), 0)
    images = draw_images(jax.random.fold_in(splits[6], 71), 0)
    pair_group = jnp.searchsorted(jnp.cumsum(uneven(splits[3], B_TOTAL // 2, B_TOTAL, 4, 0)), jnp.arange(B_TOTAL), side="right").astype(jnp.int32)
    w_up = centred(splits[4], (D, FF), D ** -0.5, 0.1875, ((1, 2),))
    w_down = centred(splits[5], (D, FF), FF ** -0.5, 0.09375, ((1, 2),))
    return {"tokens": tokens, "lengths": lengths, "images": images, "pair_group": pair_group, "w_up": w_up, "w_down": w_down}


LOGIT_SCALE = 117.0
LOGIT_SHIFT = -12.9

def layer_norm(rows):
    center = rows - lax.optimization_barrier(jnp.mean(rows, -1, keepdims=True))
    spread = lax.optimization_barrier(jnp.mean(center * center, -1, keepdims=True))
    return center * lax.rsqrt(spread + 1e-06)

def gelu_pair(pre):
    const = 0.7978845608028654
    inner = const * (pre + 0.044715 * pre * pre * pre)
    tanh_u = jnp.tanh(inner)
    value = 0.5 * pre * (1.0 + tanh_u)
    slope = 0.5 * (1.0 + tanh_u) + 0.5 * pre * (1.0 - tanh_u * tanh_u) * const * (1.0 + 3.0 * 0.044715 * pre * pre)
    return (value, slope)

def front(tok_block, len_block, w_up):
    captions = len_block.shape[0]
    seq_len = tok_block.shape[0] // captions
    tok_float = tok_block.astype(jnp.float32)
    normed = layer_norm(tok_float).astype(jnp.bfloat16)
    pre = jnp.dot(normed, w_up, preferred_element_type=jnp.float32)
    value, slope = gelu_pair(pre)
    position = jnp.arange(seq_len, dtype=jnp.int32)
    valid = (position[None, :] < len_block[:, None]).astype(jnp.float32)
    share = valid / lax.optimization_barrier(jnp.sum(valid, 1, keepdims=True))
    return (normed, value, slope, share, tok_float)

def unit_rows(rows):
    scale = lax.rsqrt(lax.optimization_barrier(jnp.sum(rows * rows, 1, keepdims=True)) + 1e-06)
    return (rows * scale, scale)

def reference(tokens, lengths, images, pair_group, w_up, w_down):
    blocks = B_TOTAL // B_DEV
    tok_blocks = tokens.reshape(blocks, B_DEV * TOKLEN, D)
    len_blocks = lengths.reshape(blocks, B_DEV)

    def forward(pieces):
        tok_block, len_block = pieces
        normed, value, slope, share, tok_float = front(tok_block, len_block, w_up)
        gmean = lax.optimization_barrier(jnp.sum(value.reshape(B_DEV, TOKLEN, FF) * share[:, :, None], 1))
        tmean = lax.optimization_barrier(jnp.sum(tok_float.reshape(B_DEV, TOKLEN, D) * share[:, :, None], 1))
        return (gmean, tmean)
    gmean, tmean = lax.map(forward, (tok_blocks, len_blocks))
    gbar = gmean.reshape(B_TOTAL, FF).astype(jnp.bfloat16)
    tmean = tmean.reshape(B_TOTAL, D)
    pooled = tmean + lax.dot_general(gbar, w_down, (((1,), (1,)), ((), ())), preferred_element_type=jnp.float32)
    unit_text, text_scale = unit_rows(pooled)
    unit_image, image_scale = unit_rows(images.astype(jnp.float32))
    text_half = unit_text.astype(jnp.bfloat16)
    image_half = unit_image.astype(jnp.bfloat16)
    logits = LOGIT_SCALE * lax.dot_general(text_half, image_half, (((1,), (1,)), ((), ())), preferred_element_type=jnp.float32) + LOGIT_SHIFT
    signs = jnp.where(pair_group[:, None] == pair_group[None, :], 1.0, -1.0).astype(jnp.float32)
    caption_loss = -lax.optimization_barrier(jnp.sum(jax.nn.log_sigmoid(signs * logits), 1)) / B_TOTAL
    coef = (-LOGIT_SCALE * signs * jax.nn.sigmoid(-signs * logits)).astype(jnp.bfloat16)
    text_back = jnp.dot(coef, image_half, preferred_element_type=jnp.float32)
    image_back = lax.dot_general(coef, text_half, (((0,), (0,)), ((), ())), preferred_element_type=jnp.float32)
    pooled_grad = (text_back - unit_text * lax.optimization_barrier(jnp.sum(unit_text * text_back, 1, keepdims=True))) * text_scale
    image_grad = (image_back - unit_image * lax.optimization_barrier(jnp.sum(unit_image * image_back, 1, keepdims=True))) * image_scale
    pooled_half = pooled_grad.astype(jnp.bfloat16)
    hidden_grad = jnp.dot(pooled_half, w_down, preferred_element_type=jnp.float32)
    hidden_blocks = hidden_grad.reshape(blocks, B_DEV, FF)

    def backward(total, pieces):
        tok_block, len_block, grad_block = pieces
        normed, value, slope, share, tok_float = front(tok_block, len_block, w_up)
        pre_grad = (share[:, :, None] * grad_block[:, None, :] * slope.reshape(B_DEV, TOKLEN, FF)).astype(jnp.bfloat16)
        pre_grad = pre_grad.reshape(B_DEV * TOKLEN, FF)
        term = lax.dot_general(normed, pre_grad, (((0,), (0,)), ((), ())), preferred_element_type=jnp.float32)
        return (total + term, None)
    up_grad, unused = lax.scan(backward, jnp.zeros((D, FF), jnp.float32), (tok_blocks, len_blocks, hidden_blocks))
    down_grad = lax.dot_general(pooled_half, gbar, (((0,), (0,)), ((), ())), preferred_element_type=jnp.float32)
    return (caption_loss, image_grad, up_grad, down_grad)
```

```python
import jax
import jax.numpy as jnp
from jax import lax
from jax.sharding import PartitionSpec as P

LOGIT_SCALE = 117.0
LOGIT_SHIFT = -12.9


def layer_norm(rows):
    center = rows - jnp.mean(rows, -1, keepdims=True)
    spread = jnp.mean(center * center, -1, keepdims=True)
    return center * lax.rsqrt(spread + 1e-06)


def gelu_pair(pre):
    const = 0.7978845608028654
    inner = const * (pre + 0.044715 * pre * pre * pre)
    tanh_u = jnp.tanh(inner)
    value = 0.5 * pre * (1.0 + tanh_u)
    slope = 0.5 * (1.0 + tanh_u) + 0.5 * pre * (1.0 - tanh_u * tanh_u) * const * (
        1.0 + 3.0 * 0.044715 * pre * pre
    )
    return (value, slope)


def unit_rows(rows):
    scale = lax.rsqrt(jnp.sum(rows * rows, 1, keepdims=True) + 1e-06)
    return (rows * scale, scale)


def signed_logits(text_rows, text_group, image_rows, image_group):
    logits = (
        LOGIT_SCALE
        * lax.dot_general(
            text_rows, image_rows, (((1,), (1,)), ((), ())), preferred_element_type=jnp.float32
        )
        + LOGIT_SHIFT
    )
    signs = jnp.where(text_group[:, None] == image_group[None, :], 1.0, -1.0).astype(jnp.float32)
    return (signs, signs * logits)


def loss_slope(signs, signed):
    return (-LOGIT_SCALE * signs * jax.nn.sigmoid(-signed)).astype(jnp.bfloat16)


def through_unit(back, unit, scale):
    return (back - unit * jnp.sum(unit * back, 1, keepdims=True)) * scale


def on_device(tokens, lengths, images, pair_group, w_up, w_down):
    captions = lengths.shape[0]
    seq_len = tokens.shape[0] // captions
    width = tokens.shape[1]
    hidden = w_up.shape[1]
    devices = lax.axis_size("dp")
    own_index = lax.axis_index("dp")
    total = captions * devices
    own_rows = width // devices
    own_group = lax.dynamic_slice_in_dim(pair_group, own_index * captions, captions)

    unit_image, image_scale = unit_rows(images.astype(jnp.float32))
    image_half = unit_image.astype(jnp.bfloat16)
    all_images = lax.all_gather(image_half, "dp", axis=0, tiled=True)

    tok_float = tokens.astype(jnp.float32)
    normed = layer_norm(tok_float).astype(jnp.bfloat16)
    pre = jnp.dot(normed, w_up, preferred_element_type=jnp.float32)
    value, slope = gelu_pair(pre)
    position = jnp.arange(seq_len, dtype=jnp.int32)
    valid = (position[None, :] < lengths[:, None]).astype(jnp.float32)
    share = valid / jnp.sum(valid, 1, keepdims=True)
    gmean = jnp.sum(value.reshape(captions, seq_len, hidden) * share[:, :, None], 1)
    tmean = jnp.sum(tok_float.reshape(captions, seq_len, width) * share[:, :, None], 1)
    gbar = gmean.astype(jnp.bfloat16)
    partial_value = lax.dot_general(
        gbar, w_down, (((1,), (1,)), ((), ())), preferred_element_type=jnp.float32
    )
    pooled = tmean + lax.psum(partial_value, "mp")
    unit_text, text_scale = unit_rows(pooled)
    text_half = unit_text.astype(jnp.bfloat16)

    signs, signed = signed_logits(text_half, own_group, all_images, pair_group)
    caption_loss = -jnp.sum(jax.nn.log_sigmoid(signed), 1) / total
    text_back = jnp.dot(loss_slope(signs, signed), all_images, preferred_element_type=jnp.float32)
    pooled_half = through_unit(text_back, unit_text, text_scale).astype(jnp.bfloat16)

    hidden_grad = jnp.dot(pooled_half, w_down, preferred_element_type=jnp.float32)
    pre_grad = (
        share[:, :, None] * hidden_grad[:, None, :] * slope.reshape(captions, seq_len, hidden)
    ).astype(jnp.bfloat16)
    pre_grad = pre_grad.reshape(captions * seq_len, hidden)
    up_grad = lax.psum_scatter(
        lax.dot_general(
            normed, pre_grad, (((0,), (0,)), ((), ())), preferred_element_type=jnp.float32
        ),
        "dp",
        scatter_dimension=0,
        tiled=True,
    )

    all_texts = lax.all_gather(text_half, "dp", axis=0, tiled=True)
    signs, signed = signed_logits(all_texts, pair_group, image_half, own_group)
    image_back = lax.dot_general(
        loss_slope(signs, signed), all_texts, (((0,), (0,)), ((), ())),
        preferred_element_type=jnp.float32,
    )
    image_grad = through_unit(image_back, unit_image, image_scale)
    all_gbar = lax.all_gather(gbar, "dp", axis=0, tiled=True)
    all_pooled = lax.all_gather(pooled_half, "dp", axis=0, tiled=True)
    own_pooled = lax.dynamic_slice_in_dim(all_pooled, own_index * own_rows, own_rows, 1)
    down_grad = lax.dot_general(
        own_pooled, all_gbar, (((0,), (0,)), ((), ())), preferred_element_type=jnp.float32
    )
    return (caption_loss, image_grad, up_grad, down_grad)


def solution(mesh):
    in_specs = (P("dp", None), P("dp"), P("dp", None), P(), P(None, "mp"), P(None, "mp"))
    out_specs = (P("dp"), P("dp", None), P("dp", "mp"), P("dp", "mp"))
    return jax.shard_map(
        on_device, mesh=mesh, in_specs=in_specs, out_specs=out_specs, check_vma=False
    )
```

```python
import jax
import jax.numpy as jnp
from jax import lax
from jax.experimental import pallas as pl
from jax.experimental.pallas import tpu as pltpu
from jax.sharding import PartitionSpec as P

LOGIT_SCALE = 117.0
LOGIT_SHIFT = -12.9


def layer_norm(rows):
    center = rows - jnp.mean(rows, -1, keepdims=True)
    spread = jnp.mean(center * center, -1, keepdims=True)
    return center * lax.rsqrt(spread + 1e-06)


def gelu_pair(pre):
    const = 0.7978845608028654
    inner = const * (pre + 0.044715 * pre * pre * pre)
    tanh_u = jnp.tanh(inner)
    value = 0.5 * pre * (1.0 + tanh_u)
    slope = 0.5 * (1.0 + tanh_u) + 0.5 * pre * (1.0 - tanh_u * tanh_u) * const * (
        1.0 + 3.0 * 0.044715 * pre * pre
    )
    return (value, slope)


def unit_rows(rows):
    scale = lax.rsqrt(jnp.sum(rows * rows, 1, keepdims=True) + 1e-06)
    return (rows * scale, scale)


LANES = 128
SLABS = 3
MESH = pl.DeviceIdType.MESH


def slab_width(hidden):
    return -(-hidden // (2 * SLABS * LANES)) * LANES


def sum_over_chips_kernel(
    own_ref, other_ref, grad_ref, out_ref, grad_other, keep, x_out, x_in, near_out, near_in,
    far_out, far_in, swap_out, swap_in, grad_sems, x_sems, near_sems, far_sems, swap_sems
):
    rank = lax.axis_index("dp")
    column = lax.axis_index("mp")
    core = rank % 2
    x = (rank // 2) % 2
    z = rank // 4
    low, high = z % 2, z // 2
    width = grad_other.shape[2]
    half = SLABS * width
    rows = keep.shape[2]
    own_rows = rows // 2

    def device(z_at, x_at, core_at):
        return ((z_at * 2 + x_at) * 2 + core_at, column)

    core_peer = device(z, x, 1 - core)
    x_peer = device(z, 1 - x, core)
    near_peer = device(z + 1 - 2 * low, x, core)
    far_peer = device(z + 2 - 4 * high, x, core)

    barrier = pltpu.get_barrier_semaphore()
    for peer in (core_peer, x_peer, near_peer, far_peer):
        pl.semaphore_signal(barrier, inc=1, device_id=peer, device_id_type=MESH)
    pl.semaphore_wait(barrier, 4)

    def copy(src, dst, sems, index, peer):
        return pltpu.make_async_remote_copy(
            src_ref=src,
            dst_ref=dst,
            send_sem=sems.at[0, index],
            recv_sem=sems.at[1, index],
            device_id=peer,
            device_id_type=MESH,
        )

    def columns(which, slab):
        return pl.ds(pl.multiple_of(which * half + slab * width, LANES), width)

    def grad_copy(slab):
        return copy(
            grad_ref.at[:, columns(1 - core, slab)], grad_other.at[slab], grad_sems, slab, core_peer
        )

    def x_copy(step):
        return copy(x_out.at[step], x_in.at[step], x_sems, step, x_peer)

    def near_copy(step):
        return copy(near_out.at[step], near_in.at[step], near_sems, step, near_peer)

    def far_copy(step):
        return copy(far_out.at[step], far_in.at[step], far_sems, step, far_peer)

    def swap_copy(step):
        return copy(swap_out.at[step], swap_in.at[step], swap_sems, step, core_peer)

    for slab in range(SLABS):
        grad_copy(slab).start()

    def block(d0, d1, x_at, slab):
        z_at = z + d0 * (1 - 2 * low) + d1 * (2 - 4 * high)
        at = pl.ds(pl.multiple_of((z_at * 2 + x_at) * rows, 16), rows)
        return jnp.dot(
            own_ref[at, :], grad_ref[:, columns(core, slab)], preferred_element_type=jnp.float32
        ) + jnp.dot(other_ref[at, :], grad_other[slab], preferred_element_type=jnp.float32)

    for slab in range(SLABS):
        grad_copy(slab).wait_recv()

        @pl.loop(0, 1)
        def _(unused, slab=slab):
            x_out[slab] = block(1, 1, 1 - x, slab).astype(jnp.bfloat16)
            x_copy(slab).start()

    @pl.loop(SLABS, 4 * SLABS)
    def _(step):
        turn, slab = step // SLABS, step % SLABS
        x_out[step] = block(1 - turn % 2, 1 - turn // 2, 1 - x, slab).astype(jnp.bfloat16)
        x_copy(step).start()

    @pl.loop(0, 4 * SLABS)
    def _(step):
        turn, slab = step // SLABS, step % SLABS
        keep[step // SLABS, step % SLABS] = block(1 - turn % 2, 1 - turn // 2, x, slab)

    @pl.loop(0, SLABS)
    def _(slab):
        x_copy(slab).wait_recv()
        near_out[slab] = (keep[0, slab] + x_in[slab].astype(jnp.float32)).astype(jnp.bfloat16)
        near_copy(slab).start()

    @pl.loop(0, SLABS)
    def _(slab):
        x_copy(SLABS + slab).wait_recv()
        near_copy(slab).wait_recv()
        far_out[slab] = (
            keep[1, slab]
            + x_in[SLABS + slab].astype(jnp.float32)
            + near_in[slab].astype(jnp.float32)
        ).astype(jnp.bfloat16)
        far_copy(slab).start()

    @pl.loop(0, SLABS)
    def _(slab):
        x_copy(2 * SLABS + slab).wait_recv()
        near_out[SLABS + slab] = (
            keep[2, slab] + x_in[2 * SLABS + slab].astype(jnp.float32)
        ).astype(jnp.bfloat16)
        near_copy(SLABS + slab).start()

    for slab in range(SLABS):
        x_copy(3 * SLABS + slab).wait_recv()
        near_copy(SLABS + slab).wait_recv()
        far_copy(slab).wait_recv()
        keep[3, slab] = (
            keep[3, slab]
            + x_in[3 * SLABS + slab].astype(jnp.float32)
            + near_in[SLABS + slab].astype(jnp.float32)
            + far_in[slab].astype(jnp.float32)
        )
        theirs = pl.ds(pl.multiple_of((1 - core) * own_rows, 8), own_rows)
        mine = pl.ds(pl.multiple_of(core * own_rows, 8), own_rows)
        swap_out[slab] = keep[3, slab, theirs, :]
        swap_copy(slab).start()
        out_ref[:, columns(core, slab)] = keep[3, slab, mine, :]

    for slab in range(SLABS):
        swap_copy(slab).wait_recv()
        out_ref[:, columns(1 - core, slab)] = swap_in[slab]

    for slab in range(SLABS):
        grad_copy(slab).wait_send()
        far_copy(slab).wait_send()
        swap_copy(slab).wait_send()

    @pl.loop(0, 4 * SLABS)
    def _(step):
        x_copy(step).wait_send()

    @pl.loop(0, 2 * SLABS)
    def _(step):
        near_copy(step).wait_send()


def sum_over_chips(own_t, other_t, pre_grad):
    features, tokens = own_t.shape
    width = pre_grad.shape[1] // (2 * SLABS)
    rows = features // 8
    own_rows = rows // 2
    bf16, f32 = jnp.bfloat16, jnp.float32
    vmem = pl.BlockSpec(memory_space=pltpu.VMEM)
    dma = pltpu.SemaphoreType.DMA
    flops = 4 * features * tokens * pre_grad.shape[1] // 2
    return pl.pallas_call(
        sum_over_chips_kernel,
        out_shape=jax.ShapeDtypeStruct((own_rows, pre_grad.shape[1]), f32),
        in_specs=[vmem] * 3,
        out_specs=vmem,
        scratch_shapes=[
            pltpu.VMEM((SLABS, tokens, width), bf16),
            pltpu.VMEM((4, SLABS, rows, width), f32),
            pltpu.VMEM((4 * SLABS, rows, width), bf16),
            pltpu.VMEM((4 * SLABS, rows, width), bf16),
            pltpu.VMEM((2 * SLABS, rows, width), bf16),
            pltpu.VMEM((2 * SLABS, rows, width), bf16),
            pltpu.VMEM((SLABS, rows, width), bf16),
            pltpu.VMEM((SLABS, rows, width), bf16),
            pltpu.VMEM((SLABS, own_rows, width), f32),
            pltpu.VMEM((SLABS, own_rows, width), f32),
            dma((2, SLABS)),
            dma((2, 4 * SLABS)),
            dma((2, 2 * SLABS)),
            dma((2, SLABS)),
            dma((2, SLABS)),
        ],
        cost_estimate=pl.CostEstimate(
            flops=flops, bytes_accessed=4 * features * pre_grad.shape[1], transcendentals=0
        ),
        compiler_params=pltpu.CompilerParams(
            collective_id=0, has_side_effects=True, vmem_limit_bytes=48 * 1024 * 1024
        ),
    )(own_t, other_t, pre_grad)


def signed_logits(text_rows, text_group, image_rows, image_group):
    logits = (
        LOGIT_SCALE
        * lax.dot_general(
            text_rows, image_rows, (((1,), (1,)), ((), ())), preferred_element_type=jnp.float32
        )
        + LOGIT_SHIFT
    )
    signs = jnp.where(text_group[:, None] == image_group[None, :], 1.0, -1.0).astype(jnp.float32)
    return (signs, signs * logits)


def loss_slope(signs, signed):
    return (-LOGIT_SCALE * signs * jax.nn.sigmoid(-signed)).astype(jnp.bfloat16)


def through_unit(back, unit, scale):
    return (back - unit * jnp.sum(unit * back, 1, keepdims=True)) * scale


def on_device(tokens, lengths, images, pair_group, w_up, w_down):
    captions = lengths.shape[0]
    seq_len = tokens.shape[0] // captions
    width = tokens.shape[1]
    hidden = w_up.shape[1]
    devices = lax.axis_size("dp")
    own_index = lax.axis_index("dp")
    total = captions * devices
    own_rows = width // devices
    own_group = lax.dynamic_slice_in_dim(pair_group, own_index * captions, captions)

    unit_image, image_scale = unit_rows(images.astype(jnp.float32))
    image_half = unit_image.astype(jnp.bfloat16)
    all_images = lax.all_gather(unit_image, "dp", axis=0, tiled=True)
    all_images = lax.optimization_barrier(all_images).astype(jnp.bfloat16)

    tok_float = tokens.astype(jnp.float32)
    normed = layer_norm(tok_float).astype(jnp.bfloat16)
    pre = jnp.dot(normed, w_up, preferred_element_type=jnp.float32)
    value, slope = gelu_pair(pre)
    position = jnp.arange(seq_len, dtype=jnp.int32)
    valid = (position[None, :] < lengths[:, None]).astype(jnp.float32)
    share = valid / jnp.sum(valid, 1, keepdims=True)
    gmean = jnp.sum(value.reshape(captions, seq_len, hidden) * share[:, :, None], 1)
    tmean = jnp.sum(tok_float.reshape(captions, seq_len, width) * share[:, :, None], 1)
    gbar = gmean.astype(jnp.bfloat16)
    partial_value = lax.dot_general(
        gbar, w_down, (((1,), (1,)), ((), ())), preferred_element_type=jnp.float32
    )
    pooled = tmean + lax.psum(partial_value, "mp")
    unit_text, text_scale = unit_rows(pooled)
    text_half = unit_text.astype(jnp.bfloat16)

    signs, signed = signed_logits(text_half, own_group, all_images, pair_group)
    caption_loss = -jnp.sum(jax.nn.log_sigmoid(signed), 1) / total
    text_back = jnp.dot(loss_slope(signs, signed), all_images, preferred_element_type=jnp.float32)
    pooled_half = through_unit(text_back, unit_text, text_scale).astype(jnp.bfloat16)

    gathered = lax.all_gather(
        jnp.concatenate([text_half, pooled_half, gbar], 1), "dp", axis=0, tiled=True
    )
    all_texts = gathered[:, :width]
    all_pooled = gathered[:, width : 2 * width]
    all_gbar = gathered[:, 2 * width :]

    by_chips = devices == 16 and width % 128 == 0
    if by_chips:
        padding = 2 * SLABS * slab_width(hidden) - hidden
        w_down = jnp.pad(w_down, ((0, 0), (0, padding)))
        slope = jnp.pad(slope, ((0, 0), (0, padding)))
    hidden_grad = jnp.dot(pooled_half, w_down, preferred_element_type=jnp.float32)
    pre_grad = (
        share[:, :, None] * hidden_grad[:, None, :] * slope.reshape(captions, seq_len, -1)
    ).astype(jnp.bfloat16)
    pre_grad = pre_grad.reshape(captions * seq_len, -1)
    if by_chips:
        normed_t = normed.T
        other_t = lax.ppermute(normed_t, "dp", [(i, i ^ 1) for i in range(devices)])
        up_grad = sum_over_chips(normed_t, other_t, pre_grad)[:, :hidden]
    else:
        up_grad = lax.psum_scatter(
            lax.dot_general(
                normed, pre_grad, (((0,), (0,)), ((), ())), preferred_element_type=jnp.float32
            ),
            "dp",
            scatter_dimension=0,
            tiled=True,
        )

    signs, signed = signed_logits(all_texts, pair_group, image_half, own_group)
    image_back = lax.dot_general(
        loss_slope(signs, signed), all_texts, (((0,), (0,)), ((), ())),
        preferred_element_type=jnp.float32,
    )
    image_grad = through_unit(image_back, unit_image, image_scale)
    own_pooled = lax.dynamic_slice_in_dim(all_pooled, own_index * own_rows, own_rows, 1)
    down_grad = lax.dot_general(
        own_pooled, all_gbar, (((0,), (0,)), ((), ())), preferred_element_type=jnp.float32
    )
    return (caption_loss, image_grad, up_grad, down_grad)


def solution(mesh):
    in_specs = (P("dp", None), P("dp"), P("dp", None), P(), P(None, "mp"), P(None, "mp"))
    out_specs = (P("dp"), P("dp", None), P("dp", "mp"), P("dp", "mp"))
    return jax.shard_map(
        on_device, mesh=mesh, in_specs=in_specs, out_specs=out_specs, check_vma=False
    )
```

```python
import functools

import jax
import jax.numpy as jnp
from jax import lax
from jax.experimental import pallas as pl
from jax.experimental.pallas import tpu as pltpu
from jax.sharding import PartitionSpec as P

LOGIT_SCALE = 117.0
LOGIT_SHIFT = -12.9


def layer_norm(rows):
    center = rows - jnp.mean(rows, -1, keepdims=True)
    spread = jnp.mean(center * center, -1, keepdims=True)
    return center * lax.rsqrt(spread + 1e-06)


def gelu_pair(pre):
    const = 0.7978845608028654
    square = pre * pre
    half = 0.5 + 0.5 * jnp.tanh(pre * (const + const * 0.044715 * square))
    value = pre * half
    slope = half + value * (1.0 - half) * (2.0 * const + 6.0 * const * 0.044715 * square)
    return (value, slope)


def unit_rows(rows):
    scale = lax.rsqrt(jnp.sum(rows * rows, 1, keepdims=True) + 1e-06)
    return (rows * scale, scale)


def signed_logits(text_rows, text_group, image_rows, image_group):
    logits = (
        LOGIT_SCALE
        * lax.dot_general(
            text_rows, image_rows, (((1,), (1,)), ((), ())), preferred_element_type=jnp.float32
        )
        + LOGIT_SHIFT
    )
    signs = jnp.where(text_group == image_group, 1.0, -1.0).astype(jnp.float32)
    return (signs, signs * logits)


def loss_slope(signs, signed):
    return (-LOGIT_SCALE * signs * jax.nn.sigmoid(-signed)).astype(jnp.bfloat16)


def through_unit(back, unit, scale):
    return (back - unit * jnp.sum(unit * back, 1, keepdims=True)) * scale


LANES = 128
SLABS = 3
MESH = pl.DeviceIdType.MESH


def slab_width(hidden):
    return -(-hidden // (2 * SLABS * LANES)) * LANES


class Place:
    def __init__(self):
        rank = lax.axis_index("dp")
        self.column = lax.axis_index("mp")
        self.rank = rank
        self.core = rank % 2
        self.x = (rank // 2) % 2
        self.z = rank // 4
        self.low, self.high = self.z % 2, self.z // 2

    def toward(self, far, near, across, other):
        z = self.z + far * (2 - 4 * self.high) + near * (1 - 2 * self.low)
        x = self.x + across * (1 - 2 * self.x)
        core = self.core + other * (1 - 2 * self.core)
        return (z * 2 + x) * 2 + core

    def peer(self, *flips):
        return (self.toward(*flips), self.column)

    def mp_peer(self):
        return (self.rank, 1 - self.column)


def meet(peers):
    barrier = pltpu.get_barrier_semaphore()
    for peer in peers:
        pl.semaphore_signal(barrier, inc=1, device_id=peer, device_id_type=MESH)
    pl.semaphore_wait(barrier, len(peers))


def remote(src, dst, sems, index, peer):
    return pltpu.make_async_remote_copy(
        src_ref=src,
        dst_ref=dst,
        send_sem=sems.at[0, index],
        recv_sem=sems.at[1, index],
        device_id=peer,
        device_id_type=MESH,
    )


def forward_kernel(
    total, tok_ref, share_ref, img_ref, group_ref, own_group_ref, up_hbm, down_hbm,
    gbar_ref, text_ref, pooled_ref, loss_ref, hidden_ref, slope_ref, own_t, other_t,
    w_up, w_down, normed, pre_a, pre_b, gmean, tmean, images, mine, theirs,
    local_sems, img_sems, mp_sems, t_sems
):
    place = Place()
    captions = gbar_ref.shape[0]
    hidden = gbar_ref.shape[1]
    tokens = tok_ref.shape[0]
    seq_len = tokens // captions
    width = slab_width(hidden)
    tile = tokens // 2
    tile_captions = captions // 2
    last = hidden // width * width
    f32, bf16 = jnp.float32, jnp.bfloat16

    up_copy = pltpu.make_async_copy(up_hbm, w_up, local_sems.at[0])
    down_copy = pltpu.make_async_copy(down_hbm, w_down, local_sems.at[1])
    up_copy.start()
    down_copy.start()

    unit, unused = unit_rows(img_ref[...].astype(f32))

    def block_of(rank):
        return pl.ds(pl.multiple_of(rank * captions, 16), captions)

    images[block_of(place.rank), :] = unit.astype(bf16)
    far, near, across, core = (1, 0, 0, 0), (0, 1, 0, 0), (0, 0, 1, 0), (0, 0, 0, 1)
    meet([place.peer(*far), place.peer(*near), place.peer(*across), place.peer(*core),
          place.mp_peer()])

    stages = (far, near, across, core)

    def img_copies(stage):
        copies = []
        for held in range(1 << stage):
            flips = [(held >> bit) & 1 if bit < stage else 0 for bit in range(4)]
            at = block_of(place.toward(*flips))
            copies.append(
                remote(images.at[at, :], images.at[at, :], img_sems, (1 << stage) - 1 + held,
                       place.peer(*stages[stage]))
            )
        return copies

    def img_start(stage):
        for c in img_copies(stage):
            c.start()

    def img_wait(stage):
        for c in img_copies(stage):
            c.wait_recv()

    img_start(0)

    @pl.loop(0, 2)
    def _(turn):
        at = pl.ds(pl.multiple_of(turn * tile, 16), tile)
        tok = tok_ref[at, :].astype(f32)
        normed[at, :] = layer_norm(tok).astype(bf16)
        shared = (tok * share_ref[at, 0:1]).reshape(tile_captions, seq_len, tok.shape[1])
        tmean[pl.ds(pl.multiple_of(turn * tile_captions, 8), tile_captions), :] = jnp.sum(
            shared, 1
        )

    img_wait(0)
    img_start(1)
    up_copy.wait()

    def project(dst, turn, cols, size):
        dst[:, :size] = jnp.dot(
            normed[turn * tile : (turn + 1) * tile, :], w_up[:, cols], preferred_element_type=f32
        )

    def activate(src, turn, cols, size):
        rows = slice(turn * tile, (turn + 1) * tile)
        value, slope = gelu_pair(src[:, :size])
        slope_ref[rows, cols] = slope
        shared = (value * share_ref[rows, 0:1]).reshape(tile_captions, seq_len, size)
        gmean[turn * tile_captions : (turn + 1) * tile_captions, cols] = jnp.sum(shared, 1)

    def slab_columns(slab):
        return pl.ds(pl.multiple_of(slab * width, LANES), width)

    project(pre_a, 0, slice(0, width), width)

    @pl.loop(0, last // width - 1)
    def _(slab):
        project(pre_b, 1, slab_columns(slab), width)
        activate(pre_a, 0, slab_columns(slab), width)
        project(pre_a, 0, slab_columns(slab + 1), width)
        activate(pre_b, 1, slab_columns(slab), width)

        @pl.when(slab == 0)
        def _():
            img_wait(1)
            img_start(2)

        @pl.when(slab == 2)
        def _():
            img_wait(2)
            img_start(3)

    end = slice(last - width, last)
    project(pre_b, 1, end, width)
    activate(pre_a, 0, end, width)
    if last < hidden:
        rest = slice(last, hidden)
        slope_ref[:, last:] = jnp.zeros((tokens, slope_ref.shape[1] - last), f32)
        project(pre_a, 0, rest, hidden - last)
        activate(pre_b, 1, end, width)
        project(pre_b, 1, rest, hidden - last)
        activate(pre_a, 0, rest, hidden - last)
        activate(pre_b, 1, rest, hidden - last)
    else:
        activate(pre_b, 1, end, width)

    gbar_ref[...] = gmean[:, :hidden].astype(bf16)
    down_copy.wait()
    mine[...] = lax.dot_general(
        gbar_ref[...], w_down[...], (((1,), (1,)), ((), ())), preferred_element_type=f32
    )
    mp_copy = remote(mine, theirs, mp_sems, 0, place.mp_peer())
    mp_copy.start()
    for turn in range(2):
        own_t[:, turn * tile : (turn + 1) * tile] = normed[turn * tile : (turn + 1) * tile, :].T
    t_copy = remote(own_t, other_t, t_sems, 0, place.peer(*core))
    t_copy.start()
    img_wait(3)
    mp_copy.wait_recv()
    pooled = tmean[...] + (mine[...] + theirs[...])
    unit_text, text_scale = unit_rows(pooled)
    text_half = unit_text.astype(bf16)
    text_ref[...] = text_half
    signs, signed = signed_logits(text_half, own_group_ref[...], images[...], group_ref[...])
    loss = jnp.sum(jnp.maximum(-signed, 0.0) + jnp.log1p(jnp.exp(-jnp.abs(signed))), 1, keepdims=True)
    loss_ref[...] = jnp.broadcast_to(loss / total, loss_ref.shape)
    text_back = jnp.dot(loss_slope(signs, signed), images[...], preferred_element_type=f32)
    pooled_half = through_unit(text_back, unit_text, text_scale).astype(bf16)
    pooled_ref[...] = pooled_half
    hidden_ref[:, last:] = jnp.zeros((captions, hidden_ref.shape[1] - last), f32)
    hidden_ref[:, :hidden] = jnp.dot(pooled_half, w_down[...], preferred_element_type=f32)

    for stage in range(4):
        for c in img_copies(stage):
            c.wait_send()
    mp_copy.wait_send()
    t_copy.wait()


def forward(tokens, share, images, pair_group, own_group, w_up, w_down, total):
    count, width = tokens.shape
    captions = images.shape[0]
    hidden = w_up.shape[1]
    slab = slab_width(hidden)
    bf16, f32 = jnp.bfloat16, jnp.float32
    vmem = pl.BlockSpec(memory_space=pltpu.VMEM)
    hbm = pl.BlockSpec(memory_space=pl.ANY)
    dma = pltpu.SemaphoreType.DMA
    shape = jax.ShapeDtypeStruct
    return pl.pallas_call(
        functools.partial(forward_kernel, total),
        out_shape=(
            shape((captions, hidden), bf16),
            shape((captions, width), bf16),
            shape((captions, width), bf16),
            shape((captions, LANES), f32),
            shape((captions, 2 * SLABS * slab), f32),
            shape((count, 2 * SLABS * slab), f32),
            shape((width, count), bf16),
            shape((width, count), bf16),
        ),
        in_specs=[vmem] * 5 + [hbm] * 2,
        out_specs=(vmem,) * 8,
        scratch_shapes=[
            pltpu.VMEM(w_up.shape, bf16),
            pltpu.VMEM(w_down.shape, bf16),
            pltpu.VMEM((count, width), bf16),
            pltpu.VMEM((count // 2, slab), f32),
            pltpu.VMEM((count // 2, slab), f32),
            pltpu.VMEM((captions, 2 * SLABS * slab), f32),
            pltpu.VMEM((captions, width), f32),
            pltpu.VMEM((total, width), bf16),
            pltpu.VMEM((captions, width), f32),
            pltpu.VMEM((captions, width), f32),
            dma((2,)),
            dma((2, 15)),
            dma((2, 1)),
            dma((2, 1)),
        ],
        cost_estimate=pl.CostEstimate(
            flops=2 * count * width * hidden, bytes_accessed=4 * count * hidden,
            transcendentals=count * hidden,
        ),
        compiler_params=pltpu.CompilerParams(
            collective_id=1, has_side_effects=True, vmem_limit_bytes=56 * 1024 * 1024
        ),
    )(
        tokens,
        share,
        images,
        pair_group.reshape(1, total),
        own_group.reshape(captions, 1),
        w_up,
        w_down,
    )


def sum_over_chips_kernel(
    own_ref, other_ref, hidden_ref, share_ref, slope_ref, out_ref, grad_ref, grad_other, keep, x_out, x_in, near_out, near_in,
    far_out, far_in, swap_out, swap_in, grad_sems, x_sems, near_sems, far_sems, swap_sems
):
    rank = lax.axis_index("dp")
    column = lax.axis_index("mp")
    core = rank % 2
    x = (rank // 2) % 2
    z = rank // 4
    low, high = z % 2, z // 2
    width = grad_other.shape[2]
    half = SLABS * width
    rows = keep.shape[2]
    own_rows = rows // 2

    def device(z_at, x_at, core_at):
        return ((z_at * 2 + x_at) * 2 + core_at, column)

    core_peer = device(z, x, 1 - core)
    x_peer = device(z, 1 - x, core)
    near_peer = device(z + 1 - 2 * low, x, core)
    far_peer = device(z + 2 - 4 * high, x, core)

    barrier = pltpu.get_barrier_semaphore()
    for peer in (core_peer, x_peer, near_peer, far_peer):
        pl.semaphore_signal(barrier, inc=1, device_id=peer, device_id_type=MESH)
    pl.semaphore_wait(barrier, 4)

    def copy(src, dst, sems, index, peer):
        return pltpu.make_async_remote_copy(
            src_ref=src,
            dst_ref=dst,
            send_sem=sems.at[0, index],
            recv_sem=sems.at[1, index],
            device_id=peer,
            device_id_type=MESH,
        )

    def columns(which, slab):
        return pl.ds(pl.multiple_of(which * half + slab * width, LANES), width)

    def grad_copy(slab):
        return copy(
            grad_ref.at[:, columns(1 - core, slab)], grad_other.at[slab], grad_sems, slab, core_peer
        )

    def x_copy(step):
        return copy(x_out.at[step], x_in.at[step], x_sems, step, x_peer)

    def near_copy(step):
        return copy(near_out.at[step], near_in.at[step], near_sems, step, near_peer)

    def far_copy(step):
        return copy(far_out.at[step], far_in.at[step], far_sems, step, far_peer)

    def swap_copy(step):
        return copy(swap_out.at[step], swap_in.at[step], swap_sems, step, core_peer)

    tokens = grad_ref.shape[0]
    captions = hidden_ref.shape[0]
    tile, tile_captions = tokens // 2, captions // 2

    def make_grad(which, slab):
        cols = columns(which, slab)
        for turn in range(2):
            at = slice(turn * tile, (turn + 1) * tile)
            of = slice(turn * tile_captions, (turn + 1) * tile_captions)
            shape = (tile_captions, tokens // captions, width)
            hidden = jnp.broadcast_to(hidden_ref[of, cols][:, None, :], shape).reshape(tile, width)
            grad = share_ref[at, 0:1] * hidden * slope_ref[at, cols]
            grad_ref[at, cols] = grad.astype(jnp.bfloat16)

    @pl.loop(0, SLABS)
    def _(slab):
        make_grad(1 - core, slab)
        grad_copy(slab).start()

    @pl.loop(0, SLABS)
    def _(slab):
        make_grad(core, slab)

    def block(d0, d1, x_at, slab):
        z_at = z + d0 * (1 - 2 * low) + d1 * (2 - 4 * high)
        at = pl.ds(pl.multiple_of((z_at * 2 + x_at) * rows, 16), rows)
        return jnp.dot(
            own_ref[at, :], grad_ref[:, columns(core, slab)], preferred_element_type=jnp.float32
        ) + jnp.dot(other_ref[at, :], grad_other[slab], preferred_element_type=jnp.float32)

    for slab in range(SLABS):
        grad_copy(slab).wait_recv()

        @pl.loop(0, 1)
        def _(unused, slab=slab):
            x_out[slab] = block(1, 1, 1 - x, slab).astype(jnp.bfloat16)
            x_copy(slab).start()

    @pl.loop(SLABS, 4 * SLABS)
    def _(step):
        turn, slab = step // SLABS, step % SLABS
        x_out[step] = block(1 - turn % 2, 1 - turn // 2, 1 - x, slab).astype(jnp.bfloat16)
        x_copy(step).start()

    @pl.loop(0, 4 * SLABS)
    def _(step):
        turn, slab = step // SLABS, step % SLABS
        keep[step // SLABS, step % SLABS] = block(1 - turn % 2, 1 - turn // 2, x, slab)

    @pl.loop(0, SLABS)
    def _(slab):
        x_copy(slab).wait_recv()
        near_out[slab] = (keep[0, slab] + x_in[slab].astype(jnp.float32)).astype(jnp.bfloat16)
        near_copy(slab).start()

    @pl.loop(0, SLABS)
    def _(slab):
        x_copy(SLABS + slab).wait_recv()
        near_copy(slab).wait_recv()
        far_out[slab] = (
            keep[1, slab]
            + x_in[SLABS + slab].astype(jnp.float32)
            + near_in[slab].astype(jnp.float32)
        ).astype(jnp.bfloat16)
        far_copy(slab).start()

    @pl.loop(0, SLABS)
    def _(slab):
        x_copy(2 * SLABS + slab).wait_recv()
        near_out[SLABS + slab] = (
            keep[2, slab] + x_in[2 * SLABS + slab].astype(jnp.float32)
        ).astype(jnp.bfloat16)
        near_copy(SLABS + slab).start()

    for slab in range(SLABS):
        x_copy(3 * SLABS + slab).wait_recv()
        near_copy(SLABS + slab).wait_recv()
        far_copy(slab).wait_recv()
        keep[3, slab] = (
            keep[3, slab]
            + x_in[3 * SLABS + slab].astype(jnp.float32)
            + near_in[SLABS + slab].astype(jnp.float32)
            + far_in[slab].astype(jnp.float32)
        )
        theirs = pl.ds(pl.multiple_of((1 - core) * own_rows, 8), own_rows)
        mine = pl.ds(pl.multiple_of(core * own_rows, 8), own_rows)
        swap_out[slab] = keep[3, slab, theirs, :]
        swap_copy(slab).start()
        out_ref[:, columns(core, slab)] = keep[3, slab, mine, :]

    for slab in range(SLABS):
        swap_copy(slab).wait_recv()
        out_ref[:, columns(1 - core, slab)] = swap_in[slab]

    for slab in range(SLABS):
        grad_copy(slab).wait_send()
        far_copy(slab).wait_send()
        swap_copy(slab).wait_send()

    @pl.loop(0, 4 * SLABS)
    def _(step):
        x_copy(step).wait_send()

    @pl.loop(0, 2 * SLABS)
    def _(step):
        near_copy(step).wait_send()


def sum_over_chips(own_t, other_t, hidden_grad, share, slope):
    features, tokens = own_t.shape
    width = slope.shape[1] // (2 * SLABS)
    rows = features // 8
    own_rows = rows // 2
    bf16, f32 = jnp.bfloat16, jnp.float32
    vmem = pl.BlockSpec(memory_space=pltpu.VMEM)
    dma = pltpu.SemaphoreType.DMA
    flops = 4 * features * tokens * slope.shape[1] // 2
    return pl.pallas_call(
        sum_over_chips_kernel,
        out_shape=jax.ShapeDtypeStruct((own_rows, slope.shape[1]), f32),
        in_specs=[vmem] * 5,
        out_specs=vmem,
        scratch_shapes=[
            pltpu.VMEM(slope.shape, bf16),
            pltpu.VMEM((SLABS, tokens, width), bf16),
            pltpu.VMEM((4, SLABS, rows, width), f32),
            pltpu.VMEM((4 * SLABS, rows, width), bf16),
            pltpu.VMEM((4 * SLABS, rows, width), bf16),
            pltpu.VMEM((2 * SLABS, rows, width), bf16),
            pltpu.VMEM((2 * SLABS, rows, width), bf16),
            pltpu.VMEM((SLABS, rows, width), bf16),
            pltpu.VMEM((SLABS, rows, width), bf16),
            pltpu.VMEM((SLABS, own_rows, width), f32),
            pltpu.VMEM((SLABS, own_rows, width), f32),
            dma((2, SLABS)),
            dma((2, 4 * SLABS)),
            dma((2, 2 * SLABS)),
            dma((2, SLABS)),
            dma((2, SLABS)),
        ],
        cost_estimate=pl.CostEstimate(
            flops=flops, bytes_accessed=4 * features * slope.shape[1], transcendentals=0
        ),
        compiler_params=pltpu.CompilerParams(
            collective_id=0, has_side_effects=True, vmem_limit_bytes=56 * 1024 * 1024
        ),
    )(own_t, other_t, hidden_grad, share, slope)


def on_device(tokens, lengths, images, pair_group, w_up, w_down):
    captions = lengths.shape[0]
    seq_len = tokens.shape[0] // captions
    width = tokens.shape[1]
    hidden = w_up.shape[1]
    devices = lax.axis_size("dp")
    own_index = lax.axis_index("dp")
    total = captions * devices
    own_rows = width // devices
    own_group = lax.dynamic_slice_in_dim(pair_group, own_index * captions, captions)
    position = jnp.arange(seq_len, dtype=jnp.int32)
    valid = (position[None, :] < lengths[:, None]).astype(jnp.float32)
    share = valid / jnp.sum(valid, 1, keepdims=True)
    unit_image, image_scale = unit_rows(images.astype(jnp.float32))
    image_half = unit_image.astype(jnp.bfloat16)

    by_chips = devices == 16 and lax.axis_size("mp") == 2 and captions == 16
    if by_chips:
        share = jnp.broadcast_to(share.reshape(captions * seq_len, 1), (captions * seq_len, LANES))
        gbar, text_half, pooled_half, loss, hidden_grad, slope, own_t, other_t = forward(
            tokens, share, images, pair_group, own_group, w_up, w_down, total
        )
        caption_loss = loss[:, 0]
    else:
        all_images = lax.all_gather(image_half, "dp", axis=0, tiled=True)
        tok_float = tokens.astype(jnp.float32)
        normed = layer_norm(tok_float).astype(jnp.bfloat16)
        pre = jnp.dot(normed, w_up, preferred_element_type=jnp.float32)
        value, slope = gelu_pair(pre)
        gmean = jnp.sum(value.reshape(captions, seq_len, hidden) * share[:, :, None], 1)
        tmean = jnp.sum(tok_float.reshape(captions, seq_len, width) * share[:, :, None], 1)
        gbar = gmean.astype(jnp.bfloat16)
        partial_value = lax.dot_general(
            gbar, w_down, (((1,), (1,)), ((), ())), preferred_element_type=jnp.float32
        )
        pooled = tmean + lax.psum(partial_value, "mp")
        unit_text, text_scale = unit_rows(pooled)
        text_half = unit_text.astype(jnp.bfloat16)
        signs, signed = signed_logits(
            text_half, own_group[:, None], all_images, pair_group[None, :]
        )
        caption_loss = -jnp.sum(jax.nn.log_sigmoid(signed), 1) / total
        text_back = jnp.dot(
            loss_slope(signs, signed), all_images, preferred_element_type=jnp.float32
        )
        pooled_half = through_unit(text_back, unit_text, text_scale).astype(jnp.bfloat16)

    gathered = lax.all_gather(
        jnp.concatenate([text_half, pooled_half, gbar], 1), "dp", axis=0, tiled=True
    )
    all_texts = gathered[:, :width]
    all_pooled = gathered[:, width : 2 * width]
    all_gbar = gathered[:, 2 * width :]

    if by_chips:
        up_grad = sum_over_chips(own_t, other_t, hidden_grad, share, slope)[:, :hidden]
    else:
        hidden_grad = jnp.dot(pooled_half, w_down, preferred_element_type=jnp.float32)
        pre_grad = (
            share[:, :, None] * hidden_grad[:, None, :] * slope.reshape(captions, seq_len, hidden)
        ).astype(jnp.bfloat16)
        pre_grad = pre_grad.reshape(captions * seq_len, hidden)
        up_grad = lax.psum_scatter(
            lax.dot_general(
                normed, pre_grad, (((0,), (0,)), ((), ())), preferred_element_type=jnp.float32
            ),
            "dp",
            scatter_dimension=0,
            tiled=True,
        )

    signs, signed = signed_logits(
        all_texts, pair_group[:, None], image_half, own_group[None, :]
    )
    image_back = lax.dot_general(
        loss_slope(signs, signed), all_texts, (((0,), (0,)), ((), ())),
        preferred_element_type=jnp.float32,
    )
    image_grad = through_unit(image_back, unit_image, image_scale)
    own_pooled = lax.dynamic_slice_in_dim(all_pooled, own_index * own_rows, own_rows, 1)
    down_grad = lax.dot_general(
        own_pooled, all_gbar, (((0,), (0,)), ((), ())), preferred_element_type=jnp.float32
    )
    return (caption_loss, image_grad, up_grad, down_grad)


def solution(mesh):
    in_specs = (P("dp", None), P("dp"), P("dp", None), P(), P(None, "mp"), P(None, "mp"))
    out_specs = (P("dp"), P("dp", None), P("dp", "mp"), P("dp", "mp"))
    return jax.shard_map(
        on_device, mesh=mesh, in_specs=in_specs, out_specs=out_specs, check_vma=False
    )
```

```python
import functools

import jax
import jax.numpy as jnp
from jax import lax
from jax.experimental import pallas as pl
from jax.experimental.pallas import tpu as pltpu
from jax.sharding import PartitionSpec as P

LOGIT_SCALE = 117.0
LOGIT_SHIFT = -12.9


def layer_norm(rows):
    center = rows - jnp.mean(rows, -1, keepdims=True)
    spread = jnp.mean(center * center, -1, keepdims=True)
    return center * lax.rsqrt(spread + 1e-06)


def gelu_pair(pre):
    const = 0.7978845608028654
    square = pre * pre
    half = 0.5 + 0.5 * jnp.tanh(pre * (const + const * 0.044715 * square))
    value = pre * half
    slope = half + value * (1.0 - half) * (2.0 * const + 6.0 * const * 0.044715 * square)
    return (value, slope)


def unit_rows(rows):
    scale = lax.rsqrt(jnp.sum(rows * rows, 1, keepdims=True) + 1e-06)
    return (rows * scale, scale)


def signed_logits(text_rows, text_group, image_rows, image_group):
    logits = (
        LOGIT_SCALE
        * lax.dot_general(
            text_rows, image_rows, (((1,), (1,)), ((), ())), preferred_element_type=jnp.float32
        )
        + LOGIT_SHIFT
    )
    signs = jnp.where(text_group == image_group, 1.0, -1.0).astype(jnp.float32)
    return (signs, signs * logits)


def loss_slope(signs, signed):
    return (-LOGIT_SCALE * signs * jax.nn.sigmoid(-signed)).astype(jnp.bfloat16)


def through_unit(back, unit, scale):
    return (back - unit * jnp.sum(unit * back, 1, keepdims=True)) * scale


LANES = 128
SLABS = 3
MESH = pl.DeviceIdType.MESH


def slab_width(hidden):
    return -(-hidden // (2 * SLABS * LANES)) * LANES


class Place:
    def __init__(self):
        rank = lax.axis_index("dp")
        self.column = lax.axis_index("mp")
        self.rank = rank
        self.core = rank % 2
        self.x = (rank // 2) % 2
        self.z = rank // 4
        self.low, self.high = self.z % 2, self.z // 2

    def toward(self, far, near, across, other):
        z = self.z + far * (2 - 4 * self.high) + near * (1 - 2 * self.low)
        x = self.x + across * (1 - 2 * self.x)
        core = self.core + other * (1 - 2 * self.core)
        return (z * 2 + x) * 2 + core

    def peer(self, *flips):
        return (self.toward(*flips), self.column)

    def mp_peer(self):
        return (self.rank, 1 - self.column)


def meet(peers):
    barrier = pltpu.get_barrier_semaphore()
    for peer in peers:
        pl.semaphore_signal(barrier, inc=1, device_id=peer, device_id_type=MESH)
    pl.semaphore_wait(barrier, len(peers))


def remote(src, dst, sems, index, peer):
    return pltpu.make_async_remote_copy(
        src_ref=src,
        dst_ref=dst,
        send_sem=sems.at[0, index],
        recv_sem=sems.at[1, index],
        device_id=peer,
        device_id_type=MESH,
    )


def forward_kernel(
    total, tok_ref, share_ref, img_ref, group_ref, own_group_ref, up_hbm, down_hbm,
    gbar_ref, text_ref, pooled_ref, loss_ref, hidden_ref, slope_ref, own_t, other_t,
    w_up, w_down, normed, pre_a, pre_b, gmean, tmean, images, mine, theirs,
    local_sems, img_sems, mp_sems, t_sems
):
    place = Place()
    captions = gbar_ref.shape[0]
    hidden = gbar_ref.shape[1]
    tokens = tok_ref.shape[0]
    seq_len = tokens // captions
    width = slab_width(hidden)
    tile = tokens // 2
    tile_captions = captions // 2
    last = hidden // width * width
    f32, bf16 = jnp.float32, jnp.bfloat16

    up_copy = pltpu.make_async_copy(up_hbm, w_up, local_sems.at[0])
    down_copy = pltpu.make_async_copy(down_hbm, w_down, local_sems.at[1])
    up_copy.start()
    down_copy.start()

    unit, unused = unit_rows(img_ref[...].astype(f32))

    def block_of(rank):
        return pl.ds(pl.multiple_of(rank * captions, 16), captions)

    images[block_of(place.rank), :] = unit.astype(bf16)
    far, near, across, core = (1, 0, 0, 0), (0, 1, 0, 0), (0, 0, 1, 0), (0, 0, 0, 1)
    meet([place.peer(*far), place.peer(*near), place.peer(*across), place.peer(*core),
          place.mp_peer()])

    stages = (far, near, across, core)

    def img_copies(stage):
        copies = []
        for held in range(1 << stage):
            flips = [(held >> bit) & 1 if bit < stage else 0 for bit in range(4)]
            at = block_of(place.toward(*flips))
            copies.append(
                remote(images.at[at, :], images.at[at, :], img_sems, (1 << stage) - 1 + held,
                       place.peer(*stages[stage]))
            )
        return copies

    def img_start(stage):
        for c in img_copies(stage):
            c.start()

    def img_wait(stage):
        for c in img_copies(stage):
            c.wait_recv()

    img_start(0)

    @pl.loop(0, 2)
    def _(turn):
        at = pl.ds(pl.multiple_of(turn * tile, 16), tile)
        tok = tok_ref[at, :].astype(f32)
        normed[at, :] = layer_norm(tok).astype(bf16)
        shared = (tok * share_ref[at, 0:1]).reshape(tile_captions, seq_len, tok.shape[1])
        tmean[pl.ds(pl.multiple_of(turn * tile_captions, 8), tile_captions), :] = jnp.sum(
            shared, 1
        )

    img_wait(0)
    img_start(1)
    up_copy.wait()

    def project(dst, turn, cols, size):
        dst[:, :size] = lax.dot_general(
            normed[turn * tile : (turn + 1) * tile, :], w_up[cols, :], (((1,), (1,)), ((), ())),
            preferred_element_type=f32,
        )

    def activate(src, turn, cols, size):
        rows = slice(turn * tile, (turn + 1) * tile)
        value, slope = gelu_pair(src[:, :size])
        slope_ref[rows, cols] = slope
        shared = (value * share_ref[rows, 0:1]).reshape(tile_captions, seq_len, size)
        gmean[turn * tile_captions : (turn + 1) * tile_captions, cols] = jnp.sum(shared, 1)

    def slab_columns(slab):
        return pl.ds(pl.multiple_of(slab * width, LANES), width)

    project(pre_a, 0, slice(0, width), width)

    @pl.loop(0, last // width - 1)
    def _(slab):
        project(pre_b, 1, slab_columns(slab), width)
        activate(pre_a, 0, slab_columns(slab), width)
        project(pre_a, 0, slab_columns(slab + 1), width)
        activate(pre_b, 1, slab_columns(slab), width)

        @pl.when(slab == 0)
        def _():
            img_wait(1)
            img_start(2)

        @pl.when(slab == 2)
        def _():
            img_wait(2)
            img_start(3)

    end = slice(last - width, last)
    project(pre_b, 1, end, width)
    activate(pre_a, 0, end, width)
    if last < hidden:
        rest = slice(last, hidden)
        slope_ref[:, last:] = jnp.zeros((tokens, slope_ref.shape[1] - last), f32)
        project(pre_a, 0, rest, hidden - last)
        activate(pre_b, 1, end, width)
        project(pre_b, 1, rest, hidden - last)
        activate(pre_a, 0, rest, hidden - last)
        activate(pre_b, 1, rest, hidden - last)
    else:
        activate(pre_b, 1, end, width)

    gbar_ref[...] = gmean[:, :hidden].astype(bf16)
    down_copy.wait()
    mine[...] = jnp.dot(gbar_ref[...], w_down[...], preferred_element_type=f32)
    mp_copy = remote(mine, theirs, mp_sems, 0, place.mp_peer())
    mp_copy.start()
    for turn in range(2):
        own_t[:, turn * tile : (turn + 1) * tile] = normed[turn * tile : (turn + 1) * tile, :].T
    t_copy = remote(own_t, other_t, t_sems, 0, place.peer(*core))
    t_copy.start()
    img_wait(3)
    mp_copy.wait_recv()
    pooled = tmean[...] + (mine[...] + theirs[...])
    unit_text, text_scale = unit_rows(pooled)
    text_half = unit_text.astype(bf16)
    text_ref[...] = text_half
    signs, signed = signed_logits(text_half, own_group_ref[...], images[...], group_ref[...])
    loss = jnp.sum(jnp.maximum(-signed, 0.0) + jnp.log1p(jnp.exp(-jnp.abs(signed))), 1, keepdims=True)
    loss_ref[...] = jnp.broadcast_to(loss / total, loss_ref.shape)
    text_back = jnp.dot(loss_slope(signs, signed), images[...], preferred_element_type=f32)
    pooled_half = through_unit(text_back, unit_text, text_scale).astype(bf16)
    pooled_ref[...] = pooled_half
    hidden_ref[:, last:] = jnp.zeros((captions, hidden_ref.shape[1] - last), f32)
    hidden_ref[:, :hidden] = lax.dot_general(
        pooled_half, w_down[...], (((1,), (1,)), ((), ())), preferred_element_type=f32
    )

    for stage in range(4):
        for c in img_copies(stage):
            c.wait_send()
    mp_copy.wait_send()
    t_copy.wait()


def forward(tokens, share, images, pair_group, own_group, w_up, w_down, total):
    count, width = tokens.shape
    captions = images.shape[0]
    hidden = w_up.shape[0]
    slab = slab_width(hidden)
    bf16, f32 = jnp.bfloat16, jnp.float32
    vmem = pl.BlockSpec(memory_space=pltpu.VMEM)
    hbm = pl.BlockSpec(memory_space=pl.ANY)
    dma = pltpu.SemaphoreType.DMA
    shape = jax.ShapeDtypeStruct
    return pl.pallas_call(
        functools.partial(forward_kernel, total),
        out_shape=(
            shape((captions, hidden), bf16),
            shape((captions, width), bf16),
            shape((captions, width), bf16),
            shape((captions, LANES), f32),
            shape((captions, 2 * SLABS * slab), f32),
            shape((count, 2 * SLABS * slab), f32),
            shape((width, count), bf16),
            shape((width, count), bf16),
        ),
        in_specs=[vmem] * 5 + [hbm] * 2,
        out_specs=(vmem,) * 8,
        scratch_shapes=[
            pltpu.VMEM(w_up.shape, bf16),
            pltpu.VMEM(w_down.shape, bf16),
            pltpu.VMEM((count, width), bf16),
            pltpu.VMEM((count // 2, slab), f32),
            pltpu.VMEM((count // 2, slab), f32),
            pltpu.VMEM((captions, 2 * SLABS * slab), f32),
            pltpu.VMEM((captions, width), f32),
            pltpu.VMEM((total, width), bf16),
            pltpu.VMEM((captions, width), f32),
            pltpu.VMEM((captions, width), f32),
            dma((2,)),
            dma((2, 15)),
            dma((2, 1)),
            dma((2, 1)),
        ],
        cost_estimate=pl.CostEstimate(
            flops=2 * count * width * hidden, bytes_accessed=4 * count * hidden,
            transcendentals=count * hidden,
        ),
        compiler_params=pltpu.CompilerParams(
            collective_id=1, has_side_effects=True, vmem_limit_bytes=56 * 1024 * 1024
        ),
    )(
        tokens,
        share,
        images,
        pair_group.reshape(1, total),
        own_group.reshape(captions, 1),
        w_up,
        w_down,
    )


def sum_over_chips_kernel(
    own_ref, other_ref, hidden_ref, share_ref, slope_ref, out_ref, grad_ref, grad_other, keep, x_out, x_in, near_out, near_in,
    far_out, far_in, swap_out, swap_in, grad_sems, x_sems, near_sems, far_sems, swap_sems
):
    rank = lax.axis_index("dp")
    column = lax.axis_index("mp")
    core = rank % 2
    x = (rank // 2) % 2
    z = rank // 4
    low, high = z % 2, z // 2
    width = grad_other.shape[2]
    half = SLABS * width
    rows = keep.shape[2]
    own_rows = rows // 2

    def device(z_at, x_at, core_at):
        return ((z_at * 2 + x_at) * 2 + core_at, column)

    core_peer = device(z, x, 1 - core)
    x_peer = device(z, 1 - x, core)
    near_peer = device(z + 1 - 2 * low, x, core)
    far_peer = device(z + 2 - 4 * high, x, core)

    barrier = pltpu.get_barrier_semaphore()
    for peer in (core_peer, x_peer, near_peer, far_peer):
        pl.semaphore_signal(barrier, inc=1, device_id=peer, device_id_type=MESH)
    pl.semaphore_wait(barrier, 4)

    def copy(src, dst, sems, index, peer):
        return pltpu.make_async_remote_copy(
            src_ref=src,
            dst_ref=dst,
            send_sem=sems.at[0, index],
            recv_sem=sems.at[1, index],
            device_id=peer,
            device_id_type=MESH,
        )

    def columns(which, slab):
        return pl.ds(pl.multiple_of(which * half + slab * width, LANES), width)

    def grad_copy(slab):
        return copy(
            grad_ref.at[:, columns(1 - core, slab)], grad_other.at[slab], grad_sems, slab, core_peer
        )

    def x_copy(step):
        return copy(x_out.at[step], x_in.at[step], x_sems, step, x_peer)

    def near_copy(step):
        return copy(near_out.at[step], near_in.at[step], near_sems, step, near_peer)

    def far_copy(step):
        return copy(far_out.at[step], far_in.at[step], far_sems, step, far_peer)

    def swap_copy(step):
        return copy(swap_out.at[step], swap_in.at[step], swap_sems, step, core_peer)

    tokens = grad_ref.shape[0]
    captions = hidden_ref.shape[0]
    tile, tile_captions = tokens // 2, captions // 2

    def make_grad(which, slab):
        cols = columns(which, slab)
        for turn in range(2):
            at = slice(turn * tile, (turn + 1) * tile)
            of = slice(turn * tile_captions, (turn + 1) * tile_captions)
            shape = (tile_captions, tokens // captions, width)
            hidden = jnp.broadcast_to(hidden_ref[of, cols][:, None, :], shape).reshape(tile, width)
            grad = share_ref[at, 0:1] * hidden * slope_ref[at, cols]
            grad_ref[at, cols] = grad.astype(jnp.bfloat16)

    @pl.loop(0, SLABS)
    def _(slab):
        make_grad(1 - core, slab)
        grad_copy(slab).start()

    @pl.loop(0, SLABS)
    def _(slab):
        make_grad(core, slab)

    def block(d0, d1, x_at, slab):
        z_at = z + d0 * (1 - 2 * low) + d1 * (2 - 4 * high)
        at = pl.ds(pl.multiple_of((z_at * 2 + x_at) * rows, 16), rows)
        return jnp.dot(
            own_ref[at, :], grad_ref[:, columns(core, slab)], preferred_element_type=jnp.float32
        ) + jnp.dot(other_ref[at, :], grad_other[slab], preferred_element_type=jnp.float32)

    for slab in range(SLABS):
        grad_copy(slab).wait_recv()

        @pl.loop(0, 1)
        def _(unused, slab=slab):
            x_out[slab] = block(1, 1, 1 - x, slab).astype(jnp.bfloat16)
            x_copy(slab).start()

    @pl.loop(SLABS, 4 * SLABS)
    def _(step):
        turn, slab = step // SLABS, step % SLABS
        x_out[step] = block(1 - turn % 2, 1 - turn // 2, 1 - x, slab).astype(jnp.bfloat16)
        x_copy(step).start()

    @pl.loop(0, 4 * SLABS)
    def _(step):
        turn, slab = step // SLABS, step % SLABS
        keep[step // SLABS, step % SLABS] = block(1 - turn % 2, 1 - turn // 2, x, slab)

    @pl.loop(0, SLABS)
    def _(slab):
        x_copy(slab).wait_recv()
        near_out[slab] = (keep[0, slab] + x_in[slab].astype(jnp.float32)).astype(jnp.bfloat16)
        near_copy(slab).start()

    @pl.loop(0, SLABS)
    def _(slab):
        x_copy(SLABS + slab).wait_recv()
        near_copy(slab).wait_recv()
        far_out[slab] = (
            keep[1, slab]
            + x_in[SLABS + slab].astype(jnp.float32)
            + near_in[slab].astype(jnp.float32)
        ).astype(jnp.bfloat16)
        far_copy(slab).start()

    @pl.loop(0, SLABS)
    def _(slab):
        x_copy(2 * SLABS + slab).wait_recv()
        near_out[SLABS + slab] = (
            keep[2, slab] + x_in[2 * SLABS + slab].astype(jnp.float32)
        ).astype(jnp.bfloat16)
        near_copy(SLABS + slab).start()

    for slab in range(SLABS):
        x_copy(3 * SLABS + slab).wait_recv()
        near_copy(SLABS + slab).wait_recv()
        far_copy(slab).wait_recv()
        keep[3, slab] = (
            keep[3, slab]
            + x_in[3 * SLABS + slab].astype(jnp.float32)
            + near_in[SLABS + slab].astype(jnp.float32)
            + far_in[slab].astype(jnp.float32)
        )
        theirs = pl.ds(pl.multiple_of((1 - core) * own_rows, 8), own_rows)
        mine = pl.ds(pl.multiple_of(core * own_rows, 8), own_rows)
        swap_out[slab] = keep[3, slab, theirs, :]
        swap_copy(slab).start()
        out_ref[:, columns(core, slab)] = keep[3, slab, mine, :]

    for slab in range(SLABS):
        swap_copy(slab).wait_recv()
        out_ref[:, columns(1 - core, slab)] = swap_in[slab]

    for slab in range(SLABS):
        grad_copy(slab).wait_send()
        far_copy(slab).wait_send()
        swap_copy(slab).wait_send()

    @pl.loop(0, 4 * SLABS)
    def _(step):
        x_copy(step).wait_send()

    @pl.loop(0, 2 * SLABS)
    def _(step):
        near_copy(step).wait_send()


def sum_over_chips(own_t, other_t, hidden_grad, share, slope):
    features, tokens = own_t.shape
    width = slope.shape[1] // (2 * SLABS)
    rows = features // 8
    own_rows = rows // 2
    bf16, f32 = jnp.bfloat16, jnp.float32
    vmem = pl.BlockSpec(memory_space=pltpu.VMEM)
    dma = pltpu.SemaphoreType.DMA
    flops = 4 * features * tokens * slope.shape[1] // 2
    return pl.pallas_call(
        sum_over_chips_kernel,
        out_shape=jax.ShapeDtypeStruct((own_rows, slope.shape[1]), f32),
        in_specs=[vmem] * 5,
        out_specs=vmem,
        scratch_shapes=[
            pltpu.VMEM(slope.shape, bf16),
            pltpu.VMEM((SLABS, tokens, width), bf16),
            pltpu.VMEM((4, SLABS, rows, width), f32),
            pltpu.VMEM((4 * SLABS, rows, width), bf16),
            pltpu.VMEM((4 * SLABS, rows, width), bf16),
            pltpu.VMEM((2 * SLABS, rows, width), bf16),
            pltpu.VMEM((2 * SLABS, rows, width), bf16),
            pltpu.VMEM((SLABS, rows, width), bf16),
            pltpu.VMEM((SLABS, rows, width), bf16),
            pltpu.VMEM((SLABS, own_rows, width), f32),
            pltpu.VMEM((SLABS, own_rows, width), f32),
            dma((2, SLABS)),
            dma((2, 4 * SLABS)),
            dma((2, 2 * SLABS)),
            dma((2, SLABS)),
            dma((2, SLABS)),
        ],
        cost_estimate=pl.CostEstimate(
            flops=flops, bytes_accessed=4 * features * slope.shape[1], transcendentals=0
        ),
        compiler_params=pltpu.CompilerParams(
            collective_id=0, has_side_effects=True, vmem_limit_bytes=56 * 1024 * 1024
        ),
    )(own_t, other_t, hidden_grad, share, slope)


def on_device(tokens, lengths, images, pair_group, w_up, w_down):
    captions = lengths.shape[0]
    seq_len = tokens.shape[0] // captions
    width = tokens.shape[1]
    hidden = w_up.shape[1]
    devices = lax.axis_size("dp")
    own_index = lax.axis_index("dp")
    total = captions * devices
    own_rows = width // devices
    own_group = lax.dynamic_slice_in_dim(pair_group, own_index * captions, captions)
    position = jnp.arange(seq_len, dtype=jnp.int32)
    valid = (position[None, :] < lengths[:, None]).astype(jnp.float32)
    share = valid / jnp.sum(valid, 1, keepdims=True)
    unit_image, image_scale = unit_rows(images.astype(jnp.float32))
    image_half = unit_image.astype(jnp.bfloat16)

    by_chips = devices == 16 and lax.axis_size("mp") == 2 and captions == 16
    if by_chips:
        share = jnp.broadcast_to(share.reshape(captions * seq_len, 1), (captions * seq_len, LANES))
        gbar, text_half, pooled_half, loss, hidden_grad, slope, own_t, other_t = forward(
            tokens, share, images, pair_group, own_group, w_up.T, w_down.T, total
        )
        caption_loss = loss[:, 0]
    else:
        all_images = lax.all_gather(image_half, "dp", axis=0, tiled=True)
        tok_float = tokens.astype(jnp.float32)
        normed = layer_norm(tok_float).astype(jnp.bfloat16)
        pre = jnp.dot(normed, w_up, preferred_element_type=jnp.float32)
        value, slope = gelu_pair(pre)
        gmean = jnp.sum(value.reshape(captions, seq_len, hidden) * share[:, :, None], 1)
        tmean = jnp.sum(tok_float.reshape(captions, seq_len, width) * share[:, :, None], 1)
        gbar = gmean.astype(jnp.bfloat16)
        partial_value = lax.dot_general(
            gbar, w_down, (((1,), (1,)), ((), ())), preferred_element_type=jnp.float32
        )
        pooled = tmean + lax.psum(partial_value, "mp")
        unit_text, text_scale = unit_rows(pooled)
        text_half = unit_text.astype(jnp.bfloat16)
        signs, signed = signed_logits(
            text_half, own_group[:, None], all_images, pair_group[None, :]
        )
        caption_loss = -jnp.sum(jax.nn.log_sigmoid(signed), 1) / total
        text_back = jnp.dot(
            loss_slope(signs, signed), all_images, preferred_element_type=jnp.float32
        )
        pooled_half = through_unit(text_back, unit_text, text_scale).astype(jnp.bfloat16)

    gathered = lax.all_gather(
        jnp.concatenate([text_half, pooled_half, gbar], 1), "dp", axis=0, tiled=True
    )
    all_texts = gathered[:, :width]
    all_pooled = gathered[:, width : 2 * width]
    all_gbar = gathered[:, 2 * width :]

    if by_chips:
        up_grad = sum_over_chips(own_t, other_t, hidden_grad, share, slope)[:, :hidden]
    else:
        hidden_grad = jnp.dot(pooled_half, w_down, preferred_element_type=jnp.float32)
        pre_grad = (
            share[:, :, None] * hidden_grad[:, None, :] * slope.reshape(captions, seq_len, hidden)
        ).astype(jnp.bfloat16)
        pre_grad = pre_grad.reshape(captions * seq_len, hidden)
        up_grad = lax.psum_scatter(
            lax.dot_general(
                normed, pre_grad, (((0,), (0,)), ((), ())), preferred_element_type=jnp.float32
            ),
            "dp",
            scatter_dimension=0,
            tiled=True,
        )

    signs, signed = signed_logits(
        all_texts, pair_group[:, None], image_half, own_group[None, :]
    )
    image_back = lax.dot_general(
        loss_slope(signs, signed), all_texts, (((0,), (0,)), ((), ())),
        preferred_element_type=jnp.float32,
    )
    image_grad = through_unit(image_back, unit_image, image_scale)
    own_pooled = lax.dynamic_slice_in_dim(all_pooled, own_index * own_rows, own_rows, 1)
    down_grad = lax.dot_general(
        own_pooled, all_gbar, (((0,), (0,)), ((), ())), preferred_element_type=jnp.float32
    )
    return (caption_loss, image_grad, up_grad, down_grad)


def solution(mesh):
    in_specs = (P("dp", None), P("dp"), P("dp", None), P(), P(None, "mp"), P(None, "mp"))
    out_specs = (P("dp"), P("dp", None), P("dp", "mp"), P("dp", "mp"))
    return jax.shard_map(
        on_device, mesh=mesh, in_specs=in_specs, out_specs=out_specs, check_vma=False
    )
```

```python
import functools

import jax
import jax.numpy as jnp
from jax import lax
from jax.experimental import pallas as pl
from jax.experimental.pallas import tpu as pltpu
from jax.sharding import PartitionSpec as P

LOGIT_SCALE = 117.0
LOGIT_SHIFT = -12.9


def layer_norm(rows):
    center = rows - jnp.mean(rows, -1, keepdims=True)
    spread = jnp.mean(center * center, -1, keepdims=True)
    return center * lax.rsqrt(spread + 1e-06)


def gelu_pair(pre):
    const = 0.7978845608028654
    square = pre * pre
    half = 0.5 + 0.5 * jnp.tanh(pre * (const + const * 0.044715 * square))
    value = pre * half
    slope = half + value * (1.0 - half) * (2.0 * const + 6.0 * const * 0.044715 * square)
    return (value, slope)


def unit_rows(rows):
    scale = lax.rsqrt(jnp.sum(rows * rows, 1, keepdims=True) + 1e-06)
    return (rows * scale, scale)


def signed_logits(text_rows, text_group, image_rows, image_group):
    logits = (
        LOGIT_SCALE
        * lax.dot_general(
            text_rows, image_rows, (((1,), (1,)), ((), ())), preferred_element_type=jnp.float32
        )
        + LOGIT_SHIFT
    )
    signs = jnp.where(text_group == image_group, 1.0, -1.0).astype(jnp.float32)
    return (signs, signs * logits)


def loss_slope(signs, signed):
    return (-LOGIT_SCALE * signs * jax.nn.sigmoid(-signed)).astype(jnp.bfloat16)


def through_unit(back, unit, scale):
    return (back - unit * jnp.sum(unit * back, 1, keepdims=True)) * scale


LANES = 128
SLABS = 3
MESH = pl.DeviceIdType.MESH


def slab_width(hidden):
    return -(-hidden // (2 * SLABS * LANES)) * LANES


class Place:
    def __init__(self):
        rank = lax.axis_index("dp")
        self.column = lax.axis_index("mp")
        self.rank = rank
        self.core = rank % 2
        self.x = (rank // 2) % 2
        self.z = rank // 4
        self.low, self.high = self.z % 2, self.z // 2

    def toward(self, far, near, across, other):
        z = self.z + far * (2 - 4 * self.high) + near * (1 - 2 * self.low)
        x = self.x + across * (1 - 2 * self.x)
        core = self.core + other * (1 - 2 * self.core)
        return (z * 2 + x) * 2 + core

    def peer(self, *flips):
        return (self.toward(*flips), self.column)

    def mp_peer(self):
        return (self.rank, 1 - self.column)


def meet(peers):
    barrier = pltpu.get_barrier_semaphore()
    for peer in peers:
        pl.semaphore_signal(barrier, inc=1, device_id=peer, device_id_type=MESH)
    pl.semaphore_wait(barrier, len(peers))


def remote(src, dst, sems, index, peer):
    return pltpu.make_async_remote_copy(
        src_ref=src,
        dst_ref=dst,
        send_sem=sems.at[0, index],
        recv_sem=sems.at[1, index],
        device_id=peer,
        device_id_type=MESH,
    )


def whole_kernel(
    total, tok_ref, share_ref, img_ref, group_ref, own_group_ref, group_col_ref, own_row_ref,
    up_hbm, down_hbm,
    loss_ref, img_grad_ref, out_ref, all_pooled, all_gbar,
    all_text, hidden_ref, slope_ref, own_t, other_t,
    w_up, w_down, normed, pre_a, pre_b, gmean, tmean, images, mine, theirs,
    grad_ref, grad_other, keep, x_out, x_in, near_out, near_in, far_out, far_in, swap_out, swap_in,
    local_sems, img_sems, mp_sems, t_sems, gbar_sems, text_sems, pooled_sems,
    grad_sems, x_sems, near_sems, far_sems, swap_sems
):
    place = Place()
    captions = img_ref.shape[0]
    hidden = w_up.shape[0]
    tokens = tok_ref.shape[0]
    seq_len = tokens // captions
    width = slab_width(hidden)
    tile = tokens // 2
    tile_captions = captions // 2
    last = hidden // width * width
    f32, bf16 = jnp.float32, jnp.bfloat16

    up_copy = pltpu.make_async_copy(up_hbm, w_up, local_sems.at[0])
    down_copy = pltpu.make_async_copy(down_hbm, w_down, local_sems.at[1])
    up_copy.start()
    down_copy.start()

    unit, unused = unit_rows(img_ref[...].astype(f32))

    def block_of(rank):
        return pl.ds(pl.multiple_of(rank * captions, 16), captions)

    images[block_of(place.rank), :] = unit.astype(bf16)
    far, near, across, core = (1, 0, 0, 0), (0, 1, 0, 0), (0, 0, 1, 0), (0, 0, 0, 1)
    meet([place.peer(*far), place.peer(*near), place.peer(*across), place.peer(*core),
          place.mp_peer()])

    stages = (far, near, across, core)

    class Gather:
        def __init__(self, ref, sems):
            self.ref, self.sems = ref, sems

        def copies(self, stage):
            result = []
            for held in range(1 << stage):
                flips = [(held >> bit) & 1 if bit < stage else 0 for bit in range(4)]
                part = self.ref.at[block_of(place.toward(*flips)), :]
                index = (1 << stage) - 1 + held
                result.append(remote(part, part, self.sems, index, place.peer(*stages[stage])))
            return result

        def start(self, stage):
            for c in self.copies(stage):
                c.start()

        def wait(self, stage):
            for c in self.copies(stage):
                c.wait_recv()

        def wait_sent(self):
            for stage in range(4):
                for c in self.copies(stage):
                    c.wait_send()

    img, gbars = Gather(images, img_sems), Gather(all_gbar, gbar_sems)
    texts, pooleds = Gather(all_text, text_sems), Gather(all_pooled, pooled_sems)

    img.start(0)

    @pl.loop(0, 2)
    def _(turn):
        at = pl.ds(pl.multiple_of(turn * tile, 16), tile)
        tok = tok_ref[at, :].astype(f32)
        normed[at, :] = layer_norm(tok).astype(bf16)
        shared = (tok * share_ref[at, 0:1]).reshape(tile_captions, seq_len, tok.shape[1])
        tmean[pl.ds(pl.multiple_of(turn * tile_captions, 8), tile_captions), :] = jnp.sum(
            shared, 1
        )

    img.wait(0)
    img.start(1)
    up_copy.wait()

    def project(dst, turn, cols, size):
        dst[:, :size] = lax.dot_general(
            normed[turn * tile : (turn + 1) * tile, :], w_up[cols, :], (((1,), (1,)), ((), ())),
            preferred_element_type=f32,
        )

    def activate(src, turn, cols, size):
        rows = slice(turn * tile, (turn + 1) * tile)
        value, slope = gelu_pair(src[:, :size])
        slope_ref[rows, cols] = slope
        shared = (value * share_ref[rows, 0:1]).reshape(tile_captions, seq_len, size)
        gmean[turn * tile_captions : (turn + 1) * tile_captions, cols] = jnp.sum(shared, 1)

    def slab_columns(slab):
        return pl.ds(pl.multiple_of(slab * width, LANES), width)

    project(pre_a, 0, slice(0, width), width)

    @pl.loop(0, last // width - 1)
    def _(slab):
        project(pre_b, 1, slab_columns(slab), width)
        activate(pre_a, 0, slab_columns(slab), width)
        project(pre_a, 0, slab_columns(slab + 1), width)
        activate(pre_b, 1, slab_columns(slab), width)

        @pl.when(slab == 0)
        def _():
            img.wait(1)
            img.start(2)

        @pl.when(slab == 2)
        def _():
            img.wait(2)
            img.start(3)

    end = slice(last - width, last)
    project(pre_b, 1, end, width)
    activate(pre_a, 0, end, width)
    if last < hidden:
        rest = slice(last, hidden)
        slope_ref[:, last:] = jnp.zeros((tokens, slope_ref.shape[1] - last), f32)
        project(pre_a, 0, rest, hidden - last)
        activate(pre_b, 1, end, width)
        project(pre_b, 1, rest, hidden - last)
        activate(pre_a, 0, rest, hidden - last)
        activate(pre_b, 1, rest, hidden - last)
    else:
        activate(pre_b, 1, end, width)

    gbar = gmean[:, :hidden].astype(bf16)
    all_gbar[block_of(place.rank), :] = gbar
    gbars.start(0)
    down_copy.wait()
    mine[...] = jnp.dot(gbar, w_down[...], preferred_element_type=f32)
    mp_copy = remote(mine, theirs, mp_sems, 0, place.mp_peer())
    mp_copy.start()
    for turn in range(2):
        own_t[:, turn * tile : (turn + 1) * tile] = normed[turn * tile : (turn + 1) * tile, :].T
    t_copy = remote(own_t, other_t, t_sems, 0, place.peer(*core))
    t_copy.start()
    gbars.wait(0)
    gbars.start(1)
    img.wait(3)
    mp_copy.wait_recv()
    pooled = tmean[...] + (mine[...] + theirs[...])
    unit_text, text_scale = unit_rows(pooled)
    text_half = unit_text.astype(bf16)
    all_text[block_of(place.rank), :] = text_half
    texts.start(0)
    signs, signed = signed_logits(text_half, own_group_ref[...], images[...], group_ref[...])
    loss = jnp.sum(jnp.maximum(-signed, 0.0) + jnp.log1p(jnp.exp(-jnp.abs(signed))), 1, keepdims=True)
    loss_ref[...] = jnp.broadcast_to(loss / total, loss_ref.shape)
    text_back = jnp.dot(loss_slope(signs, signed), images[...], preferred_element_type=f32)
    pooled_half = through_unit(text_back, unit_text, text_scale).astype(bf16)
    all_pooled[block_of(place.rank), :] = pooled_half
    pooleds.start(0)
    gbars.wait(1)
    gbars.start(2)
    hidden_ref[:, last:] = jnp.zeros((captions, hidden_ref.shape[1] - last), f32)
    hidden_ref[:, :hidden] = lax.dot_general(
        pooled_half, w_down[...], (((1,), (1,)), ((), ())), preferred_element_type=f32
    )

    core, x = place.core, place.x
    low, high, z = place.low, place.high, place.z
    core_peer, x_peer = place.peer(0, 0, 0, 1), place.peer(0, 0, 1, 0)
    near_peer, far_peer = place.peer(0, 1, 0, 0), place.peer(1, 0, 0, 0)
    half = SLABS * width
    rows = keep.shape[2]
    own_rows = rows // 2
    copy = remote

    def columns(which, slab):
        return pl.ds(pl.multiple_of(which * half + slab * width, LANES), width)

    def grad_copy(slab):
        return copy(
            grad_ref.at[:, columns(1 - core, slab)], grad_other.at[slab], grad_sems, slab, core_peer
        )

    def x_copy(step):
        return copy(x_out.at[step], x_in.at[step], x_sems, step, x_peer)

    def near_copy(step):
        return copy(near_out.at[step], near_in.at[step], near_sems, step, near_peer)

    def far_copy(step):
        return copy(far_out.at[step], far_in.at[step], far_sems, step, far_peer)

    def swap_copy(step):
        return copy(swap_out.at[step], swap_in.at[step], swap_sems, step, core_peer)

    def make_grad(which, slab):
        cols = columns(which, slab)
        for turn in range(2):
            at = slice(turn * tile, (turn + 1) * tile)
            of = slice(turn * tile_captions, (turn + 1) * tile_captions)
            shape = (tile_captions, tokens // captions, width)
            hidden = jnp.broadcast_to(hidden_ref[of, cols][:, None, :], shape).reshape(tile, width)
            grad = share_ref[at, 0:1] * hidden * slope_ref[at, cols]
            grad_ref[at, cols] = grad.astype(jnp.bfloat16)

    @pl.loop(0, SLABS)
    def _(slab):
        make_grad(1 - core, slab)
        grad_copy(slab).start()

    texts.wait(0)
    texts.start(1)
    pooleds.wait(0)
    pooleds.start(1)

    @pl.loop(0, SLABS)
    def _(slab):
        make_grad(core, slab)

    texts.wait(1)
    texts.start(2)
    pooleds.wait(1)
    pooleds.start(2)
    t_copy.wait_recv()

    def block(d0, d1, x_at, slab):
        z_at = z + d0 * (1 - 2 * low) + d1 * (2 - 4 * high)
        at = pl.ds(pl.multiple_of((z_at * 2 + x_at) * rows, 16), rows)
        return jnp.dot(
            own_t[at, :], grad_ref[:, columns(core, slab)], preferred_element_type=jnp.float32
        ) + jnp.dot(other_t[at, :], grad_other[slab], preferred_element_type=jnp.float32)

    for slab in range(SLABS):
        grad_copy(slab).wait_recv()

        @pl.loop(0, 1)
        def _(unused, slab=slab):
            x_out[slab] = block(1, 1, 1 - x, slab).astype(jnp.bfloat16)
            x_copy(slab).start()

    @pl.loop(SLABS, 4 * SLABS)
    def _(step):
        turn, slab = step // SLABS, step % SLABS
        x_out[step] = block(1 - turn % 2, 1 - turn // 2, 1 - x, slab).astype(jnp.bfloat16)
        x_copy(step).start()

    @pl.loop(0, 4 * SLABS)
    def _(step):
        turn, slab = step // SLABS, step % SLABS
        keep[step // SLABS, step % SLABS] = block(1 - turn % 2, 1 - turn // 2, x, slab)

    gbars.wait(2)
    gbars.start(3)

    @pl.loop(0, SLABS)
    def _(slab):
        x_copy(slab).wait_recv()
        near_out[slab] = (keep[0, slab] + x_in[slab].astype(jnp.float32)).astype(jnp.bfloat16)
        near_copy(slab).start()

    @pl.loop(0, SLABS)
    def _(slab):
        x_copy(SLABS + slab).wait_recv()
        near_copy(slab).wait_recv()
        far_out[slab] = (
            keep[1, slab]
            + x_in[SLABS + slab].astype(jnp.float32)
            + near_in[slab].astype(jnp.float32)
        ).astype(jnp.bfloat16)
        far_copy(slab).start()

    @pl.loop(0, SLABS)
    def _(slab):
        x_copy(2 * SLABS + slab).wait_recv()
        near_out[SLABS + slab] = (
            keep[2, slab] + x_in[2 * SLABS + slab].astype(jnp.float32)
        ).astype(jnp.bfloat16)
        near_copy(SLABS + slab).start()

    texts.wait(2)
    texts.start(3)
    pooleds.wait(2)
    pooleds.start(3)
    unit_image, image_scale = unit_rows(img_ref[...].astype(f32))
    texts.wait(3)
    signs, signed = signed_logits(
        all_text[...], group_col_ref[...], unit_image.astype(bf16), own_row_ref[...]
    )
    image_back = lax.dot_general(
        loss_slope(signs, signed), all_text[...], (((0,), (0,)), ((), ())),
        preferred_element_type=f32,
    )
    img_grad_ref[...] = through_unit(image_back, unit_image, image_scale)

    for slab in range(SLABS):
        x_copy(3 * SLABS + slab).wait_recv()
        near_copy(SLABS + slab).wait_recv()
        far_copy(slab).wait_recv()
        keep[3, slab] = (
            keep[3, slab]
            + x_in[3 * SLABS + slab].astype(jnp.float32)
            + near_in[SLABS + slab].astype(jnp.float32)
            + far_in[slab].astype(jnp.float32)
        )
        theirs = pl.ds(pl.multiple_of((1 - core) * own_rows, 8), own_rows)
        mine = pl.ds(pl.multiple_of(core * own_rows, 8), own_rows)
        swap_out[slab] = keep[3, slab, theirs, :]
        swap_copy(slab).start()
        out_ref[:, columns(core, slab)] = keep[3, slab, mine, :]

    for slab in range(SLABS):
        swap_copy(slab).wait_recv()
        out_ref[:, columns(1 - core, slab)] = swap_in[slab]

    for slab in range(SLABS):
        grad_copy(slab).wait_send()
        far_copy(slab).wait_send()
        swap_copy(slab).wait_send()

    @pl.loop(0, 4 * SLABS)
    def _(step):
        x_copy(step).wait_send()

    @pl.loop(0, 2 * SLABS)
    def _(step):
        near_copy(step).wait_send()

    pooleds.wait(3)
    gbars.wait(3)
    for gather in (img, gbars, texts, pooleds):
        gather.wait_sent()
    mp_copy.wait_send()
    t_copy.wait_send()


def whole(tokens, share, images, pair_group, own_group, w_up, w_down, total):
    count, width = tokens.shape
    captions = images.shape[0]
    hidden = w_up.shape[0]
    slab = slab_width(hidden)
    padded = 2 * SLABS * slab
    rows = width // 8
    own_rows = rows // 2
    bf16, f32 = jnp.bfloat16, jnp.float32
    vmem = pl.BlockSpec(memory_space=pltpu.VMEM)
    hbm = pl.BlockSpec(memory_space=pl.ANY)
    dma = pltpu.SemaphoreType.DMA
    shape = jax.ShapeDtypeStruct
    return pl.pallas_call(
        functools.partial(whole_kernel, total),
        out_shape=(
            shape((captions, LANES), f32),
            shape((captions, width), f32),
            shape((own_rows, padded), f32),
            shape((total, width), bf16),
            shape((total, hidden), bf16),
        ),
        in_specs=[vmem] * 7 + [hbm] * 2,
        out_specs=(vmem,) * 5,
        scratch_shapes=[
            pltpu.VMEM((total, width), bf16),
            pltpu.VMEM((captions, padded), f32),
            pltpu.VMEM((count, padded), f32),
            pltpu.VMEM((width, count), bf16),
            pltpu.VMEM((width, count), bf16),
            pltpu.VMEM(w_up.shape, bf16),
            pltpu.VMEM(w_down.shape, bf16),
            pltpu.VMEM((count, width), bf16),
            pltpu.VMEM((count // 2, slab), f32),
            pltpu.VMEM((count // 2, slab), f32),
            pltpu.VMEM((captions, padded), f32),
            pltpu.VMEM((captions, width), f32),
            pltpu.VMEM((total, width), bf16),
            pltpu.VMEM((captions, width), f32),
            pltpu.VMEM((captions, width), f32),
            pltpu.VMEM((count, padded), bf16),
            pltpu.VMEM((SLABS, count, slab), bf16),
            pltpu.VMEM((4, SLABS, rows, slab), f32),
            pltpu.VMEM((4 * SLABS, rows, slab), bf16),
            pltpu.VMEM((4 * SLABS, rows, slab), bf16),
            pltpu.VMEM((2 * SLABS, rows, slab), bf16),
            pltpu.VMEM((2 * SLABS, rows, slab), bf16),
            pltpu.VMEM((SLABS, rows, slab), bf16),
            pltpu.VMEM((SLABS, rows, slab), bf16),
            pltpu.VMEM((SLABS, own_rows, slab), f32),
            pltpu.VMEM((SLABS, own_rows, slab), f32),
            dma((2,)),
            dma((2, 15)),
            dma((2, 1)),
            dma((2, 1)),
            dma((2, 15)),
            dma((2, 15)),
            dma((2, 15)),
            dma((2, SLABS)),
            dma((2, 4 * SLABS)),
            dma((2, 2 * SLABS)),
            dma((2, SLABS)),
            dma((2, SLABS)),
        ],
        cost_estimate=pl.CostEstimate(
            flops=4 * count * width * hidden, bytes_accessed=4 * width * hidden,
            transcendentals=count * hidden,
        ),
        compiler_params=pltpu.CompilerParams(
            collective_id=0, has_side_effects=True, vmem_limit_bytes=60 * 1024 * 1024
        ),
    )(
        tokens,
        share,
        images,
        pair_group.reshape(1, total),
        own_group.reshape(captions, 1),
        pair_group.reshape(total, 1),
        own_group.reshape(1, captions),
        w_up,
        w_down,
    )


def on_device(tokens, lengths, images, pair_group, w_up, w_down):
    captions = lengths.shape[0]
    seq_len = tokens.shape[0] // captions
    width = tokens.shape[1]
    hidden = w_up.shape[1]
    devices = lax.axis_size("dp")
    own_index = lax.axis_index("dp")
    total = captions * devices
    own_rows = width // devices
    own_group = lax.dynamic_slice_in_dim(pair_group, own_index * captions, captions)
    position = jnp.arange(seq_len, dtype=jnp.int32)
    valid = (position[None, :] < lengths[:, None]).astype(jnp.float32)
    share = valid / jnp.sum(valid, 1, keepdims=True)
    unit_image, image_scale = unit_rows(images.astype(jnp.float32))
    image_half = unit_image.astype(jnp.bfloat16)

    by_chips = devices == 16 and lax.axis_size("mp") == 2 and captions == 16
    if by_chips:
        share = jnp.broadcast_to(share.reshape(captions * seq_len, 1), (captions * seq_len, LANES))
        loss, image_grad, up_grad, all_pooled, all_gbar = whole(
            tokens, share, images, pair_group, own_group, w_up.T, w_down.T, total
        )
        caption_loss = loss[:, 0]
        up_grad = up_grad[:, :hidden]
    else:
        all_images = lax.all_gather(image_half, "dp", axis=0, tiled=True)
        tok_float = tokens.astype(jnp.float32)
        normed = layer_norm(tok_float).astype(jnp.bfloat16)
        pre = jnp.dot(normed, w_up, preferred_element_type=jnp.float32)
        value, slope = gelu_pair(pre)
        gmean = jnp.sum(value.reshape(captions, seq_len, hidden) * share[:, :, None], 1)
        tmean = jnp.sum(tok_float.reshape(captions, seq_len, width) * share[:, :, None], 1)
        gbar = gmean.astype(jnp.bfloat16)
        partial_value = lax.dot_general(
            gbar, w_down, (((1,), (1,)), ((), ())), preferred_element_type=jnp.float32
        )
        pooled = tmean + lax.psum(partial_value, "mp")
        unit_text, text_scale = unit_rows(pooled)
        text_half = unit_text.astype(jnp.bfloat16)
        signs, signed = signed_logits(
            text_half, own_group[:, None], all_images, pair_group[None, :]
        )
        caption_loss = -jnp.sum(jax.nn.log_sigmoid(signed), 1) / total
        text_back = jnp.dot(
            loss_slope(signs, signed), all_images, preferred_element_type=jnp.float32
        )
        pooled_half = through_unit(text_back, unit_text, text_scale).astype(jnp.bfloat16)
        hidden_grad = jnp.dot(pooled_half, w_down, preferred_element_type=jnp.float32)
        pre_grad = (
            share[:, :, None] * hidden_grad[:, None, :] * slope.reshape(captions, seq_len, hidden)
        ).astype(jnp.bfloat16)
        pre_grad = pre_grad.reshape(captions * seq_len, hidden)
        up_grad = lax.psum_scatter(
            lax.dot_general(
                normed, pre_grad, (((0,), (0,)), ((), ())), preferred_element_type=jnp.float32
            ),
            "dp",
            scatter_dimension=0,
            tiled=True,
        )
        gathered = lax.all_gather(
            jnp.concatenate([text_half, pooled_half, gbar], 1), "dp", axis=0, tiled=True
        )
        all_texts = gathered[:, :width]
        all_pooled = gathered[:, width : 2 * width]
        all_gbar = gathered[:, 2 * width :]
        unit_image, image_scale = unit_rows(images.astype(jnp.float32))
        image_half = unit_image.astype(jnp.bfloat16)
        signs, signed = signed_logits(
            all_texts, pair_group[:, None], image_half, own_group[None, :]
        )
        image_back = lax.dot_general(
            loss_slope(signs, signed), all_texts, (((0,), (0,)), ((), ())),
            preferred_element_type=jnp.float32,
        )
        image_grad = through_unit(image_back, unit_image, image_scale)

    own_pooled = lax.dynamic_slice_in_dim(all_pooled, own_index * own_rows, own_rows, 1)
    down_grad = lax.dot_general(
        own_pooled, all_gbar, (((0,), (0,)), ((), ())), preferred_element_type=jnp.float32
    )
    return (caption_loss, image_grad, up_grad, down_grad)


def solution(mesh):
    in_specs = (P("dp", None), P("dp"), P("dp", None), P(), P(None, "mp"), P(None, "mp"))
    out_specs = (P("dp"), P("dp", None), P("dp", "mp"), P("dp", "mp"))
    return jax.shard_map(
        on_device, mesh=mesh, in_specs=in_specs, out_specs=out_specs, check_vma=False
    )
```

```python
import functools

import jax
import jax.numpy as jnp
from jax import lax
from jax.experimental import pallas as pl
from jax.experimental.pallas import tpu as pltpu
from jax.sharding import PartitionSpec as P

LOGIT_SCALE = 117.0
LOGIT_SHIFT = -12.9


def layer_norm(rows):
    center = rows - jnp.mean(rows, -1, keepdims=True)
    spread = jnp.mean(center * center, -1, keepdims=True)
    return center * lax.rsqrt(spread + 1e-06)


def gelu_pair(pre):
    const = 0.7978845608028654
    square = pre * pre
    half = 0.5 + 0.5 * jnp.tanh(pre * (const + const * 0.044715 * square))
    value = pre * half
    slope = half + value * (1.0 - half) * (2.0 * const + 6.0 * const * 0.044715 * square)
    return (value, slope)


def unit_rows(rows):
    scale = lax.rsqrt(jnp.sum(rows * rows, 1, keepdims=True) + 1e-06)
    return (rows * scale, scale)


def signed_logits(text_rows, text_group, image_rows, image_group):
    logits = (
        LOGIT_SCALE
        * lax.dot_general(
            text_rows, image_rows, (((1,), (1,)), ((), ())), preferred_element_type=jnp.float32
        )
        + LOGIT_SHIFT
    )
    signs = jnp.where(text_group == image_group, 1.0, -1.0).astype(jnp.float32)
    return (signs, signs * logits)


def loss_slope(signs, signed):
    return (-LOGIT_SCALE * signs * jax.nn.sigmoid(-signed)).astype(jnp.bfloat16)


def through_unit(back, unit, scale):
    return (back - unit * jnp.sum(unit * back, 1, keepdims=True)) * scale


LANES = 128
SLABS = 3
MESH = pl.DeviceIdType.MESH


def slab_width(hidden):
    return -(-hidden // (2 * SLABS * LANES)) * LANES


class Place:
    def __init__(self):
        rank = lax.axis_index("dp")
        self.column = lax.axis_index("mp")
        self.rank = rank
        self.core = rank % 2
        self.x = (rank // 2) % 2
        self.z = rank // 4
        self.low, self.high = self.z % 2, self.z // 2

    def toward(self, far, near, across, other):
        z = self.z + far * (2 - 4 * self.high) + near * (1 - 2 * self.low)
        x = self.x + across * (1 - 2 * self.x)
        core = self.core + other * (1 - 2 * self.core)
        return (z * 2 + x) * 2 + core

    def peer(self, *flips):
        return (self.toward(*flips), self.column)

    def mp_peer(self):
        return (self.rank, 1 - self.column)


def meet(peers):
    barrier = pltpu.get_barrier_semaphore()
    for peer in peers:
        pl.semaphore_signal(barrier, inc=1, device_id=peer, device_id_type=MESH)
    pl.semaphore_wait(barrier, len(peers))


def remote(src, dst, sems, index, peer):
    return pltpu.make_async_remote_copy(
        src_ref=src,
        dst_ref=dst,
        send_sem=sems.at[0, index],
        recv_sem=sems.at[1, index],
        device_id=peer,
        device_id_type=MESH,
    )


def whole_kernel(
    total, tok_ref, len_ref, img_ref, group_ref, up_hbm, down_hbm, loss_ref, img_grad_ref, out_ref, down_ref, pooled_t, all_pooled,
    all_gbar, share_ref, all_text, hidden_ref, slope_ref, own_t, other_t,
    w_up, w_down, normed, pre_a, pre_b, gmean, tmean, images, mine, theirs,
    grad_ref, grad_other, keep, x_out, x_in, near_out, near_in, far_out, far_in, swap_out, swap_in,
    local_sems, img_sems, mp_sems, t_sems, gbar_sems, text_sems, pooled_sems,
    grad_sems, x_sems, near_sems, far_sems, swap_sems
):
    place = Place()
    captions = img_ref.shape[0]
    hidden = w_up.shape[0]
    tokens = tok_ref.shape[0]
    seq_len = tokens // captions
    width = slab_width(hidden)
    tile = tokens // 2
    tile_captions = captions // 2
    last = hidden // width * width
    rows = keep.shape[2]
    f32, bf16 = jnp.float32, jnp.bfloat16

    up_copy = pltpu.make_async_copy(up_hbm, w_up, local_sems.at[0])
    down_copy = pltpu.make_async_copy(down_hbm, w_down, local_sems.at[1])
    up_copy.start()
    down_copy.start()

    def iota(shape, dim):
        return lax.broadcasted_iota(jnp.int32, shape, dim)

    def picked(chosen, values, dim):
        return jnp.sum(jnp.where(chosen, values, 0.0), dim, keepdims=True)

    shape = (tokens, captions)
    token, caption = iota(shape, 0), iota(shape, 1)
    length = picked(token // seq_len == caption, len_ref[...].astype(f32), 1)
    position = (iota((tokens, 1), 0) % seq_len).astype(f32)
    share_ref[...] = jnp.broadcast_to(
        jnp.where(position < length, 1.0 / length, 0.0), (tokens, LANES)
    )
    groups = group_ref[...].astype(f32)
    first = place.rank * captions
    shape = (captions, total)
    own_group = picked(iota(shape, 0) + first == iota(shape, 1), groups, 1)
    group_col = picked(iota((total, total), 0) == iota((total, total), 1), groups, 1)
    shape = (total, captions)
    own_row = picked(iota(shape, 0) == iota(shape, 1) + first, group_col, 0)

    unit, unused = unit_rows(img_ref[...].astype(f32))

    def block_of(rank):
        return pl.ds(pl.multiple_of(rank * captions, 16), captions)

    images[block_of(place.rank), :] = unit.astype(bf16)
    far, near, across, core = (1, 0, 0, 0), (0, 1, 0, 0), (0, 0, 1, 0), (0, 0, 0, 1)
    meet([place.peer(*far), place.peer(*near), place.peer(*across), place.peer(*core),
          place.mp_peer()])

    stages = (far, near, across, core)

    class Gather:
        def __init__(self, ref, sems):
            self.ref, self.sems = ref, sems

        def copies(self, stage):
            result = []
            for held in range(1 << stage):
                flips = [(held >> bit) & 1 if bit < stage else 0 for bit in range(4)]
                part = self.ref.at[block_of(place.toward(*flips)), :]
                index = (1 << stage) - 1 + held
                result.append(remote(part, part, self.sems, index, place.peer(*stages[stage])))
            return result

        def start(self, stage):
            for c in self.copies(stage):
                c.start()

        def wait(self, stage):
            for c in self.copies(stage):
                c.wait_recv()

        def wait_sent(self):
            for stage in range(4):
                for c in self.copies(stage):
                    c.wait_send()

    img, gbars = Gather(images, img_sems), Gather(all_gbar, gbar_sems)
    texts, pooleds = Gather(all_text, text_sems), Gather(all_pooled, pooled_sems)

    img.start(0)

    @pl.loop(0, 2)
    def _(turn):
        at = pl.ds(pl.multiple_of(turn * tile, 16), tile)
        tok = tok_ref[at, :].astype(f32)
        normed[at, :] = layer_norm(tok).astype(bf16)
        shared = (tok * share_ref[at, 0:1]).reshape(tile_captions, seq_len, tok.shape[1])
        tmean[pl.ds(pl.multiple_of(turn * tile_captions, 8), tile_captions), :] = jnp.sum(
            shared, 1
        )

    img.wait(0)
    img.start(1)
    up_copy.wait()

    def project(dst, turn, cols, size):
        dst[:, :size] = lax.dot_general(
            normed[turn * tile : (turn + 1) * tile, :], w_up[cols, :], (((1,), (1,)), ((), ())),
            preferred_element_type=f32,
        )

    def activate(src, turn, cols, size):
        rows = slice(turn * tile, (turn + 1) * tile)
        value, slope = gelu_pair(src[:, :size])
        slope_ref[rows, cols] = slope
        shared = (value * share_ref[rows, 0:1]).reshape(tile_captions, seq_len, size)
        gmean[turn * tile_captions : (turn + 1) * tile_captions, cols] = jnp.sum(shared, 1)

    def slab_columns(slab):
        return pl.ds(pl.multiple_of(slab * width, LANES), width)

    project(pre_a, 0, slice(0, width), width)

    @pl.loop(0, last // width - 1)
    def _(slab):
        project(pre_b, 1, slab_columns(slab), width)
        activate(pre_a, 0, slab_columns(slab), width)
        project(pre_a, 0, slab_columns(slab + 1), width)
        activate(pre_b, 1, slab_columns(slab), width)

        @pl.when(slab == 0)
        def _():
            img.wait(1)
            img.start(2)

        @pl.when(slab == 2)
        def _():
            img.wait(2)
            img.start(3)

    end = slice(last - width, last)
    project(pre_b, 1, end, width)
    activate(pre_a, 0, end, width)
    if last < hidden:
        rest = slice(last, hidden)
        slope_ref[:, last:] = jnp.zeros((tokens, slope_ref.shape[1] - last), f32)
        project(pre_a, 0, rest, hidden - last)
        activate(pre_b, 1, end, width)
        project(pre_b, 1, rest, hidden - last)
        activate(pre_a, 0, rest, hidden - last)
        activate(pre_b, 1, rest, hidden - last)
    else:
        activate(pre_b, 1, end, width)

    gbar = gmean[:, :hidden].astype(bf16)
    all_gbar[block_of(place.rank), :] = gbar
    gbars.start(0)
    down_copy.wait()
    mine[...] = jnp.dot(gbar, w_down[...], preferred_element_type=f32)
    mp_copy = remote(mine, theirs, mp_sems, 0, place.mp_peer())
    mp_copy.start()
    for turn in range(2):
        turned = normed[turn * tile : (turn + 1) * tile, :].T
        for owner in range(8):
            to = (owner % 2 * 4 + owner // 2) * rows
            own_t[to : to + rows, turn * tile : (turn + 1) * tile] = turned[
                owner * rows : (owner + 1) * rows
            ]
    t_copy = remote(own_t, other_t, t_sems, 0, place.peer(*core))
    t_copy.start()
    gbars.wait(0)
    gbars.start(1)
    img.wait(3)
    mp_copy.wait_recv()
    pooled = tmean[...] + (mine[...] + theirs[...])
    unit_text, text_scale = unit_rows(pooled)
    text_half = unit_text.astype(bf16)
    all_text[block_of(place.rank), :] = text_half
    texts.start(0)
    signs, signed = signed_logits(text_half, own_group, images[...], groups)
    loss = jnp.sum(jnp.maximum(-signed, 0.0) + jnp.log1p(jnp.exp(-jnp.abs(signed))), 1, keepdims=True)
    loss_ref[...] = jnp.sum(
        jnp.where(iota((captions, captions), 0) == iota((captions, captions), 1), loss / total, 0.0),
        0, keepdims=True,
    )
    text_back = jnp.dot(loss_slope(signs, signed), images[...], preferred_element_type=f32)
    pooled_half = through_unit(text_back, unit_text, text_scale).astype(bf16)
    all_pooled[block_of(place.rank), :] = pooled_half
    pooleds.start(0)
    gbars.wait(1)
    gbars.start(2)
    hidden_ref[:, last:] = jnp.zeros((captions, hidden_ref.shape[1] - last), f32)
    hidden_ref[:, :hidden] = lax.dot_general(
        pooled_half, w_down[...], (((1,), (1,)), ((), ())), preferred_element_type=f32
    )

    core, x = place.core, place.x
    low, high, z = place.low, place.high, place.z
    core_peer, x_peer = place.peer(0, 0, 0, 1), place.peer(0, 0, 1, 0)
    near_peer, far_peer = place.peer(0, 1, 0, 0), place.peer(1, 0, 0, 0)
    half = SLABS * width
    own_rows = rows // 2
    copy = remote

    def columns(which, slab):
        return pl.ds(pl.multiple_of(which * half + slab * width, LANES), width)

    def grad_copy(slab):
        return copy(
            grad_ref.at[:, columns(1 - core, slab)], grad_other.at[slab], grad_sems, slab, core_peer
        )

    def x_copy(step):
        return copy(x_out.at[step], x_in.at[step], x_sems, step, x_peer)

    def near_copy(step):
        return copy(near_out.at[step], near_in.at[step], near_sems, step, near_peer)

    def far_copy(step):
        return copy(far_out.at[step], far_in.at[step], far_sems, step, far_peer)

    def swap_copy(step):
        return copy(swap_out.at[step], swap_in.at[step], swap_sems, step, core_peer)

    def make_grad(which, slab):
        cols = columns(which, slab)
        for turn in range(2):
            at = slice(turn * tile, (turn + 1) * tile)
            of = slice(turn * tile_captions, (turn + 1) * tile_captions)
            shape = (tile_captions, tokens // captions, width)
            hidden = jnp.broadcast_to(hidden_ref[of, cols][:, None, :], shape).reshape(tile, width)
            grad = share_ref[at, 0:1] * hidden * slope_ref[at, cols]
            grad_ref[at, cols] = grad.astype(jnp.bfloat16)

    @pl.loop(0, SLABS)
    def _(slab):
        make_grad(1 - core, slab)
        grad_copy(slab).start()

    texts.wait(0)
    texts.start(1)
    pooleds.wait(0)
    pooleds.start(1)

    @pl.loop(0, SLABS)
    def _(slab):
        make_grad(core, slab)

    texts.wait(1)
    texts.start(2)
    pooleds.wait(1)
    pooleds.start(2)
    t_copy.wait_recv()

    def z_of(turn):
        return z + (1 - turn % 2) * (1 - 2 * low) + (1 - turn // 2) * (2 - 4 * high)

    def at_x(turn, slab):
        return z_of(turn) * SLABS + slab

    def blocks(x_at, slab):
        at = pl.ds(pl.multiple_of(x_at * (4 * rows), 16), 4 * rows)
        return jnp.dot(
            own_t[at, :], grad_ref[:, columns(core, slab)], preferred_element_type=f32
        ) + jnp.dot(other_t[at, :], grad_other[slab], preferred_element_type=f32)

    @pl.loop(0, SLABS)
    def _(slab):
        grad_copy(slab).wait_recv()
        sums = blocks(1 - x, slab)
        for z_at in range(4):
            x_out[z_at * SLABS + slab] = sums[z_at * rows : (z_at + 1) * rows].astype(bf16)
        for turn in (0, 2, 1, 3):
            x_copy(at_x(turn, slab)).start()

    gbars.wait(2)
    gbars.start(3)
    texts.wait(2)
    texts.start(3)
    pooleds.wait(2)
    pooleds.start(3)

    @pl.loop(0, SLABS)
    def _(slab):
        sums = blocks(x, slab)
        for z_at in range(4):
            keep[z_at, slab] = sums[z_at * rows : (z_at + 1) * rows]

    def from_x(turn, slab):
        x_copy(at_x(turn, slab)).wait_recv()
        return keep[z_of(turn), slab] + x_in[at_x(turn, slab)].astype(f32)

    def forward_sums(slab):
        near_out[slab] = from_x(0, slab).astype(bf16)
        near_copy(slab).start()
        near_out[SLABS + slab] = from_x(2, slab).astype(bf16)
        near_copy(SLABS + slab).start()
        partial = from_x(1, slab)
        near_copy(slab).wait_recv()
        far_out[slab] = (partial + near_in[slab].astype(f32)).astype(bf16)
        far_copy(slab).start()

    def finish(slab):
        partial = from_x(3, slab)
        near_copy(SLABS + slab).wait_recv()
        far_copy(slab).wait_recv()
        keep[z, slab] = (
            partial + near_in[SLABS + slab].astype(f32) + far_in[slab].astype(f32)
        )
        peers = pl.ds(pl.multiple_of((1 - core) * own_rows, 8), own_rows)
        ours = pl.ds(pl.multiple_of(core * own_rows, 8), own_rows)
        swap_out[slab] = keep[z, slab, peers, :]
        swap_copy(slab).start()
        out_ref[:, columns(core, slab)] = keep[z, slab, ours, :]

    forward_sums(0)

    unit_image, image_scale = unit_rows(img_ref[...].astype(f32))
    texts.wait(3)
    signs, signed = signed_logits(all_text[...], group_col, unit_image.astype(bf16), own_row)
    image_back = lax.dot_general(
        loss_slope(signs, signed), all_text[...], (((0,), (0,)), ((), ())),
        preferred_element_type=f32,
    )
    img_grad_ref[...] = through_unit(image_back, unit_image, image_scale)
    pooleds.wait(3)
    gbars.wait(3)
    pooled_t[...] = all_pooled[...].astype(f32).T
    own_pooled = pooled_t[pl.ds(pl.multiple_of(place.rank * own_rows, 8), own_rows), :]
    down_ref[...] = jnp.dot(own_pooled.astype(bf16), all_gbar[...], preferred_element_type=f32)

    for slab in range(1, SLABS):
        forward_sums(slab)
        finish(slab - 1)
    finish(SLABS - 1)

    for slab in range(SLABS):
        swap_copy(slab).wait_recv()
        out_ref[:, columns(1 - core, slab)] = swap_in[slab]

    for slab in range(SLABS):
        grad_copy(slab).wait_send()
        far_copy(slab).wait_send()
        swap_copy(slab).wait_send()

    @pl.loop(0, 4 * SLABS)
    def _(step):
        x_copy(step).wait_send()

    @pl.loop(0, 2 * SLABS)
    def _(step):
        near_copy(step).wait_send()

    for gather in (img, gbars, texts, pooleds):
        gather.wait_sent()
    mp_copy.wait_send()
    t_copy.wait_send()


def whole(tokens, lengths, images, pair_group, w_up, w_down, total):
    count, width = tokens.shape
    captions = images.shape[0]
    hidden = w_up.shape[0]
    slab = slab_width(hidden)
    padded = 2 * SLABS * slab
    rows = width // 8
    own_rows = rows // 2
    bf16, f32 = jnp.bfloat16, jnp.float32
    vmem = pl.BlockSpec(memory_space=pltpu.VMEM)
    hbm = pl.BlockSpec(memory_space=pl.ANY)
    dma = pltpu.SemaphoreType.DMA
    shape = jax.ShapeDtypeStruct
    return pl.pallas_call(
        functools.partial(whole_kernel, total),
        out_shape=(
            shape((1, captions), f32),
            shape((captions, width), f32),
            shape((own_rows, padded), f32),
            shape((own_rows, hidden), f32),
        ),
        in_specs=[vmem] * 4 + [hbm] * 2,
        out_specs=(vmem,) * 4,
        scratch_shapes=[
            pltpu.VMEM((width, total), f32),
            pltpu.VMEM((total, width), bf16),
            pltpu.VMEM((total, hidden), bf16),
            pltpu.VMEM((count, LANES), f32),
            pltpu.VMEM((total, width), bf16),
            pltpu.VMEM((captions, padded), f32),
            pltpu.VMEM((count, padded), f32),
            pltpu.VMEM((width, count), bf16),
            pltpu.VMEM((width, count), bf16),
            pltpu.VMEM(w_up.shape, bf16),
            pltpu.VMEM(w_down.shape, bf16),
            pltpu.VMEM((count, width), bf16),
            pltpu.VMEM((count // 2, slab), f32),
            pltpu.VMEM((count // 2, slab), f32),
            pltpu.VMEM((captions, padded), f32),
            pltpu.VMEM((captions, width), f32),
            pltpu.VMEM((total, width), bf16),
            pltpu.VMEM((captions, width), f32),
            pltpu.VMEM((captions, width), f32),
            pltpu.VMEM((count, padded), bf16),
            pltpu.VMEM((SLABS, count, slab), bf16),
            pltpu.VMEM((4, SLABS, rows, slab), f32),
            pltpu.VMEM((4 * SLABS, rows, slab), bf16),
            pltpu.VMEM((4 * SLABS, rows, slab), bf16),
            pltpu.VMEM((2 * SLABS, rows, slab), bf16),
            pltpu.VMEM((2 * SLABS, rows, slab), bf16),
            pltpu.VMEM((SLABS, rows, slab), bf16),
            pltpu.VMEM((SLABS, rows, slab), bf16),
            pltpu.VMEM((SLABS, own_rows, slab), f32),
            pltpu.VMEM((SLABS, own_rows, slab), f32),
            dma((2,)),
            dma((2, 15)),
            dma((2, 1)),
            dma((2, 1)),
            dma((2, 15)),
            dma((2, 15)),
            dma((2, 15)),
            dma((2, SLABS)),
            dma((2, 4 * SLABS)),
            dma((2, 2 * SLABS)),
            dma((2, SLABS)),
            dma((2, SLABS)),
        ],
        cost_estimate=pl.CostEstimate(
            flops=4 * count * width * hidden, bytes_accessed=4 * width * hidden,
            transcendentals=count * hidden,
        ),
        compiler_params=pltpu.CompilerParams(
            collective_id=0, has_side_effects=True, vmem_limit_bytes=60 * 1024 * 1024
        ),
    )(
        tokens,
        lengths.reshape(1, captions),
        images,
        pair_group.reshape(1, total),
        w_up,
        w_down,
    )


def on_device(tokens, lengths, images, pair_group, w_up, w_down):
    captions = lengths.shape[0]
    seq_len = tokens.shape[0] // captions
    width = tokens.shape[1]
    hidden = w_up.shape[1]
    devices = lax.axis_size("dp")
    own_index = lax.axis_index("dp")
    total = captions * devices
    own_rows = width // devices
    own_group = lax.dynamic_slice_in_dim(pair_group, own_index * captions, captions)
    position = jnp.arange(seq_len, dtype=jnp.int32)
    valid = (position[None, :] < lengths[:, None]).astype(jnp.float32)
    share = valid / jnp.sum(valid, 1, keepdims=True)
    unit_image, image_scale = unit_rows(images.astype(jnp.float32))
    image_half = unit_image.astype(jnp.bfloat16)

    by_chips = devices == 16 and lax.axis_size("mp") == 2 and captions == 16
    if by_chips:
        loss, image_grad, up_grad, down_grad = whole(
            tokens, lengths, images, pair_group, w_up.T, w_down.T, total
        )
        caption_loss = loss.reshape(captions)
        up_grad = up_grad[:, :hidden]
    else:
        all_images = lax.all_gather(image_half, "dp", axis=0, tiled=True)
        tok_float = tokens.astype(jnp.float32)
        normed = layer_norm(tok_float).astype(jnp.bfloat16)
        pre = jnp.dot(normed, w_up, preferred_element_type=jnp.float32)
        value, slope = gelu_pair(pre)
        gmean = jnp.sum(value.reshape(captions, seq_len, hidden) * share[:, :, None], 1)
        tmean = jnp.sum(tok_float.reshape(captions, seq_len, width) * share[:, :, None], 1)
        gbar = gmean.astype(jnp.bfloat16)
        partial_value = lax.dot_general(
            gbar, w_down, (((1,), (1,)), ((), ())), preferred_element_type=jnp.float32
        )
        pooled = tmean + lax.psum(partial_value, "mp")
        unit_text, text_scale = unit_rows(pooled)
        text_half = unit_text.astype(jnp.bfloat16)
        signs, signed = signed_logits(
            text_half, own_group[:, None], all_images, pair_group[None, :]
        )
        caption_loss = -jnp.sum(jax.nn.log_sigmoid(signed), 1) / total
        text_back = jnp.dot(
            loss_slope(signs, signed), all_images, preferred_element_type=jnp.float32
        )
        pooled_half = through_unit(text_back, unit_text, text_scale).astype(jnp.bfloat16)
        hidden_grad = jnp.dot(pooled_half, w_down, preferred_element_type=jnp.float32)
        pre_grad = (
            share[:, :, None] * hidden_grad[:, None, :] * slope.reshape(captions, seq_len, hidden)
        ).astype(jnp.bfloat16)
        pre_grad = pre_grad.reshape(captions * seq_len, hidden)
        up_grad = lax.psum_scatter(
            lax.dot_general(
                normed, pre_grad, (((0,), (0,)), ((), ())), preferred_element_type=jnp.float32
            ),
            "dp",
            scatter_dimension=0,
            tiled=True,
        )
        gathered = lax.all_gather(
            jnp.concatenate([text_half, pooled_half, gbar], 1), "dp", axis=0, tiled=True
        )
        all_texts = gathered[:, :width]
        all_pooled = gathered[:, width : 2 * width]
        all_gbar = gathered[:, 2 * width :]
        unit_image, image_scale = unit_rows(images.astype(jnp.float32))
        image_half = unit_image.astype(jnp.bfloat16)
        signs, signed = signed_logits(
            all_texts, pair_group[:, None], image_half, own_group[None, :]
        )
        image_back = lax.dot_general(
            loss_slope(signs, signed), all_texts, (((0,), (0,)), ((), ())),
            preferred_element_type=jnp.float32,
        )
        image_grad = through_unit(image_back, unit_image, image_scale)
        own_pooled = lax.dynamic_slice_in_dim(all_pooled, own_index * own_rows, own_rows, 1)
        down_grad = lax.dot_general(
            own_pooled, all_gbar, (((0,), (0,)), ((), ())), preferred_element_type=jnp.float32
        )
    return (caption_loss, image_grad, up_grad, down_grad)


def solution(mesh):
    in_specs = (P("dp", None), P("dp"), P("dp", None), P(), P(None, "mp"), P(None, "mp"))
    out_specs = (P("dp"), P("dp", None), P("dp", "mp"), P("dp", "mp"))
    return jax.shard_map(
        on_device, mesh=mesh, in_specs=in_specs, out_specs=out_specs, check_vma=False
    )
```

```python
import functools

import jax
import jax.numpy as jnp
from jax import lax
from jax.experimental import pallas as pl
from jax.experimental.pallas import tpu as pltpu
from jax.sharding import PartitionSpec as P

LOGIT_SCALE = 117.0
LOGIT_SHIFT = -12.9


def layer_norm(rows):
    center = rows - jnp.mean(rows, -1, keepdims=True)
    spread = jnp.mean(center * center, -1, keepdims=True)
    return center * lax.rsqrt(spread + 1e-06)


def gelu_pair(pre):
    const = 0.7978845608028654
    square = pre * pre
    half = 0.5 + 0.5 * jnp.tanh(pre * (const + const * 0.044715 * square))
    value = pre * half
    slope = half + value * (1.0 - half) * (2.0 * const + 6.0 * const * 0.044715 * square)
    return (value, slope)


def unit_rows(rows):
    scale = lax.rsqrt(jnp.sum(rows * rows, 1, keepdims=True) + 1e-06)
    return (rows * scale, scale)


def signed_logits(text_rows, text_group, image_rows, image_group):
    logits = (
        LOGIT_SCALE
        * lax.dot_general(
            text_rows, image_rows, (((1,), (1,)), ((), ())), preferred_element_type=jnp.float32
        )
        + LOGIT_SHIFT
    )
    signs = jnp.where(text_group == image_group, 1.0, -1.0).astype(jnp.float32)
    return (signs, signs * logits)


def loss_slope(signs, signed):
    return (-LOGIT_SCALE * signs * jax.nn.sigmoid(-signed)).astype(jnp.bfloat16)


def through_unit(back, unit, scale):
    return (back - unit * jnp.sum(unit * back, 1, keepdims=True)) * scale


LANES = 128
SLABS = 3
MESH = pl.DeviceIdType.MESH


def slab_width(hidden):
    return -(-hidden // (2 * SLABS * LANES)) * LANES


class Place:
    def __init__(self):
        rank = lax.axis_index("dp")
        self.column = lax.axis_index("mp")
        self.rank = rank
        self.core = rank % 2
        self.x = (rank // 2) % 2
        self.z = rank // 4
        self.low, self.high = self.z % 2, self.z // 2

    def toward(self, far, near, across, other):
        z = self.z + far * (2 - 4 * self.high) + near * (1 - 2 * self.low)
        x = self.x + across * (1 - 2 * self.x)
        core = self.core + other * (1 - 2 * self.core)
        return (z * 2 + x) * 2 + core

    def peer(self, *flips):
        return (self.toward(*flips), self.column)

    def mp_peer(self):
        return (self.rank, 1 - self.column)


def meet(peers):
    barrier = pltpu.get_barrier_semaphore()
    for peer in peers:
        pl.semaphore_signal(barrier, inc=1, device_id=peer, device_id_type=MESH)
    pl.semaphore_wait(barrier, len(peers))


def remote(src, dst, sems, index, peer):
    return pltpu.make_async_remote_copy(
        src_ref=src,
        dst_ref=dst,
        send_sem=sems.at[0, index],
        recv_sem=sems.at[1, index],
        device_id=peer,
        device_id_type=MESH,
    )


def whole_kernel(
    total, tok_ref, len_ref, img_ref, group_ref, up_hbm, down_hbm, loss_ref, img_grad_ref, out_ref, down_ref, pooled_t, all_pooled,
    all_gbar, share_ref, all_text, hidden_ref, slope_ref, own_t, other_t,
    w_up, w_down, normed, pre_a, pre_b, gmean, tmean, images, mine, theirs,
    grad_ref, grad_other, keep, x_out, x_in, near_out, near_in, far_out, far_in, swap_out, swap_in,
    local_sems, img_sems, mp_sems, t_sems, gbar_sems, text_sems, pooled_sems,
    grad_sems, x_sems, near_sems, far_sems, swap_sems
):
    place = Place()
    captions = img_ref.shape[0]
    hidden = w_up.shape[0]
    tokens = tok_ref.shape[0]
    seq_len = tokens // captions
    width = slab_width(hidden)
    tile = tokens // 2
    tile_captions = captions // 2
    last = hidden // width * width
    rows = keep.shape[2]
    f32, bf16 = jnp.float32, jnp.bfloat16

    up_copy = pltpu.make_async_copy(up_hbm, w_up, local_sems.at[0])
    down_copy = pltpu.make_async_copy(down_hbm, w_down, local_sems.at[1])
    up_copy.start()
    down_copy.start()

    def iota(shape, dim):
        return lax.broadcasted_iota(jnp.int32, shape, dim)

    def picked(chosen, values, dim):
        return jnp.sum(jnp.where(chosen, values, 0.0), dim, keepdims=True)

    shape = (tokens, captions)
    token, caption = iota(shape, 0), iota(shape, 1)
    length = picked(token // seq_len == caption, len_ref[...].astype(f32), 1)
    position = (iota((tokens, 1), 0) % seq_len).astype(f32)
    share_ref[...] = jnp.broadcast_to(
        jnp.where(position < length, 1.0 / length, 0.0), (tokens, LANES)
    )
    groups = group_ref[...].astype(f32)
    first = place.rank * captions
    shape = (captions, total)
    own_group = picked(iota(shape, 0) + first == iota(shape, 1), groups, 1)
    group_col = picked(iota((total, total), 0) == iota((total, total), 1), groups, 1)
    shape = (total, captions)
    own_row = picked(iota(shape, 0) == iota(shape, 1) + first, group_col, 0)

    unit, unused = unit_rows(img_ref[...].astype(f32))

    def block_of(rank):
        return pl.ds(pl.multiple_of(rank * captions, 16), captions)

    images[block_of(place.rank), :] = unit.astype(bf16)
    far, near, across, core = (1, 0, 0, 0), (0, 1, 0, 0), (0, 0, 1, 0), (0, 0, 0, 1)
    meet([place.peer(*far), place.peer(*near), place.peer(*across), place.peer(*core),
          place.mp_peer()])

    stages = (far, near, across, core)

    class Gather:
        def __init__(self, ref, sems, order):
            self.ref, self.sems, self.order = ref, sems, order

        def copies(self, stage):
            result = []
            for held in range(1 << stage):
                flips = [0] * 4
                for bit in range(stage):
                    flips[self.order[bit]] = (held >> bit) & 1
                part = self.ref.at[block_of(place.toward(*flips)), :]
                index = (1 << stage) - 1 + held
                result.append(remote(part, part, self.sems, index, place.peer(*stages[self.order[stage]])))
            return result

        def start(self, stage):
            for c in self.copies(stage):
                c.start()

        def wait(self, stage):
            for c in self.copies(stage):
                c.wait_recv()

        def wait_sent(self):
            for stage in range(4):
                for c in self.copies(stage):
                    c.wait_send()

    img, gbars = Gather(images, img_sems, (0, 1, 2, 3)), Gather(all_gbar, gbar_sems, (2, 0, 1, 3))
    texts = Gather(all_text, text_sems, (0, 2, 1, 3))
    pooleds = Gather(all_pooled, pooled_sems, (0, 2, 1, 3))

    img.start(0)

    @pl.loop(0, 2)
    def _(turn):
        at = pl.ds(pl.multiple_of(turn * tile, 16), tile)
        tok = tok_ref[at, :].astype(f32)
        normed[at, :] = layer_norm(tok).astype(bf16)
        shared = (tok * share_ref[at, 0:1]).reshape(tile_captions, seq_len, tok.shape[1])
        tmean[pl.ds(pl.multiple_of(turn * tile_captions, 8), tile_captions), :] = jnp.sum(
            shared, 1
        )

    img.wait(0)
    img.start(1)
    up_copy.wait()

    def project(dst, turn, cols, size):
        dst[:, :size] = lax.dot_general(
            normed[turn * tile : (turn + 1) * tile, :], w_up[cols, :], (((1,), (1,)), ((), ())),
            preferred_element_type=f32,
        )

    def activate(src, turn, cols, size):
        rows = slice(turn * tile, (turn + 1) * tile)
        value, slope = gelu_pair(src[:, :size])
        slope_ref[rows, cols] = slope
        shared = (value * share_ref[rows, 0:1]).reshape(tile_captions, seq_len, size)
        gmean[turn * tile_captions : (turn + 1) * tile_captions, cols] = jnp.sum(shared, 1)

    def slab_columns(slab):
        return pl.ds(pl.multiple_of(slab * width, LANES), width)

    project(pre_a, 0, slice(0, width), width)

    @pl.loop(0, last // width - 1)
    def _(slab):
        project(pre_b, 1, slab_columns(slab), width)
        activate(pre_a, 0, slab_columns(slab), width)
        project(pre_a, 0, slab_columns(slab + 1), width)
        activate(pre_b, 1, slab_columns(slab), width)

        @pl.when(slab == 0)
        def _():
            img.wait(1)
            img.start(2)

        @pl.when(slab == 2)
        def _():
            img.wait(2)
            img.start(3)

    end = slice(last - width, last)
    project(pre_b, 1, end, width)
    activate(pre_a, 0, end, width)
    if last < hidden:
        rest = slice(last, hidden)
        slope_ref[:, last:] = jnp.zeros((tokens, slope_ref.shape[1] - last), f32)
        project(pre_a, 0, rest, hidden - last)
        activate(pre_b, 1, end, width)
        project(pre_b, 1, rest, hidden - last)
        activate(pre_a, 0, rest, hidden - last)
        activate(pre_b, 1, rest, hidden - last)
    else:
        activate(pre_b, 1, end, width)

    gbar = gmean[:, :hidden].astype(bf16)
    all_gbar[block_of(place.rank), :] = gbar
    gbars.start(0)
    down_copy.wait()
    mine[...] = jnp.dot(gbar, w_down[...], preferred_element_type=f32)
    mp_copy = remote(mine, theirs, mp_sems, 0, place.mp_peer())
    mp_copy.start()
    for turn in range(2):
        turned = normed[turn * tile : (turn + 1) * tile, :].T
        for owner in range(8):
            to = (owner % 2 * 4 + owner // 2) * rows
            own_t[to : to + rows, turn * tile : (turn + 1) * tile] = turned[
                owner * rows : (owner + 1) * rows
            ]
    t_copy = remote(own_t, other_t, t_sems, 0, place.peer(*core))
    t_copy.start()
    gbars.wait(0)
    gbars.start(1)
    img.wait(3)
    mp_copy.wait_recv()
    pooled = tmean[...] + (mine[...] + theirs[...])
    unit_text, text_scale = unit_rows(pooled)
    text_half = unit_text.astype(bf16)
    all_text[block_of(place.rank), :] = text_half
    texts.start(0)
    signs, signed = signed_logits(text_half, own_group, images[...], groups)
    loss = jnp.sum(jnp.maximum(-signed, 0.0) + jnp.log1p(jnp.exp(-jnp.abs(signed))), 1, keepdims=True)
    loss_ref[...] = jnp.sum(
        jnp.where(iota((captions, captions), 0) == iota((captions, captions), 1), loss / total, 0.0),
        0, keepdims=True,
    )
    text_back = jnp.dot(loss_slope(signs, signed), images[...], preferred_element_type=f32)
    pooled_half = through_unit(text_back, unit_text, text_scale).astype(bf16)
    all_pooled[block_of(place.rank), :] = pooled_half
    pooleds.start(0)
    hidden_ref[:, last:] = jnp.zeros((captions, hidden_ref.shape[1] - last), f32)
    hidden_ref[:, :hidden] = lax.dot_general(
        pooled_half, w_down[...], (((1,), (1,)), ((), ())), preferred_element_type=f32
    )

    core, x = place.core, place.x
    low, high, z = place.low, place.high, place.z
    core_peer, x_peer = place.peer(0, 0, 0, 1), place.peer(0, 0, 1, 0)
    near_peer, far_peer = place.peer(0, 1, 0, 0), place.peer(1, 0, 0, 0)
    half = SLABS * width
    own_rows = rows // 2
    copy = remote

    def columns(which, slab):
        return pl.ds(pl.multiple_of(which * half + slab * width, LANES), width)

    def grad_copy(slab):
        return copy(
            grad_ref.at[:, columns(1 - core, slab)], grad_other.at[slab], grad_sems, slab, core_peer
        )

    def x_copy(step):
        return copy(x_out.at[step], x_in.at[step], x_sems, step, x_peer)

    def near_copy(step):
        return copy(near_out.at[step], near_in.at[step], near_sems, step, near_peer)

    def far_copy(step):
        return copy(far_out.at[step], far_in.at[step], far_sems, step, far_peer)

    def swap_copy(step):
        return copy(swap_out.at[step], swap_in.at[step], swap_sems, step, core_peer)

    def make_grad(which, slab):
        cols = columns(which, slab)
        for turn in range(2):
            at = slice(turn * tile, (turn + 1) * tile)
            of = slice(turn * tile_captions, (turn + 1) * tile_captions)
            shape = (tile_captions, tokens // captions, width)
            hidden = jnp.broadcast_to(hidden_ref[of, cols][:, None, :], shape).reshape(tile, width)
            grad = share_ref[at, 0:1] * hidden * slope_ref[at, cols]
            grad_ref[at, cols] = grad.astype(jnp.bfloat16)

    @pl.loop(0, SLABS)
    def _(slab):
        make_grad(1 - core, slab)
        grad_copy(slab).start()

    texts.wait(0)
    texts.start(1)
    pooleds.wait(0)
    pooleds.start(1)
    gbars.wait(1)
    gbars.start(2)

    @pl.loop(0, SLABS)
    def _(slab):
        make_grad(core, slab)

    texts.wait(1)
    texts.start(2)
    pooleds.wait(1)
    pooleds.start(2)
    t_copy.wait_recv()

    def z_of(turn):
        return z + (1 - turn % 2) * (1 - 2 * low) + (1 - turn // 2) * (2 - 4 * high)

    def at_x(turn, slab):
        return z_of(turn) * SLABS + slab

    def blocks(x_at, slab):
        at = pl.ds(pl.multiple_of(x_at * (4 * rows), 16), 4 * rows)
        return jnp.dot(
            own_t[at, :], grad_ref[:, columns(core, slab)], preferred_element_type=f32
        ) + jnp.dot(other_t[at, :], grad_other[slab], preferred_element_type=f32)

    @pl.loop(0, SLABS)
    def _(slab):
        grad_copy(slab).wait_recv()
        sums = blocks(1 - x, slab)
        for z_at in range(4):
            x_out[z_at * SLABS + slab] = sums[z_at * rows : (z_at + 1) * rows].astype(bf16)
        for turn in (0, 2, 1, 3):
            x_copy(at_x(turn, slab)).start()

    gbars.wait(2)
    gbars.start(3)
    texts.wait(2)
    texts.start(3)
    pooleds.wait(2)
    pooleds.start(3)

    @pl.loop(0, SLABS)
    def _(slab):
        sums = blocks(x, slab)
        for z_at in range(4):
            keep[z_at, slab] = sums[z_at * rows : (z_at + 1) * rows]

    def from_x(turn, slab):
        x_copy(at_x(turn, slab)).wait_recv()
        return keep[z_of(turn), slab] + x_in[at_x(turn, slab)].astype(f32)

    def forward_sums(slab):
        near_out[slab] = from_x(0, slab).astype(bf16)
        near_copy(slab).start()
        near_out[SLABS + slab] = from_x(2, slab).astype(bf16)
        near_copy(SLABS + slab).start()
        partial = from_x(1, slab)
        near_copy(slab).wait_recv()
        far_out[slab] = (partial + near_in[slab].astype(f32)).astype(bf16)
        far_copy(slab).start()

    def finish(slab):
        partial = from_x(3, slab)
        near_copy(SLABS + slab).wait_recv()
        far_copy(slab).wait_recv()
        keep[z, slab] = (
            partial + near_in[SLABS + slab].astype(f32) + far_in[slab].astype(f32)
        )
        peers = pl.ds(pl.multiple_of((1 - core) * own_rows, 8), own_rows)
        ours = pl.ds(pl.multiple_of(core * own_rows, 8), own_rows)
        swap_out[slab] = keep[z, slab, peers, :]
        swap_copy(slab).start()
        out_ref[:, columns(core, slab)] = keep[z, slab, ours, :]

    forward_sums(0)

    unit_image, image_scale = unit_rows(img_ref[...].astype(f32))
    texts.wait(3)
    signs, signed = signed_logits(all_text[...], group_col, unit_image.astype(bf16), own_row)
    image_back = lax.dot_general(
        loss_slope(signs, signed), all_text[...], (((0,), (0,)), ((), ())),
        preferred_element_type=f32,
    )
    img_grad_ref[...] = through_unit(image_back, unit_image, image_scale)
    pooleds.wait(3)
    gbars.wait(3)
    pooled_t[...] = all_pooled[...].astype(f32).T
    own_pooled = pooled_t[pl.ds(pl.multiple_of(place.rank * own_rows, 8), own_rows), :]
    down_ref[...] = jnp.dot(own_pooled.astype(bf16), all_gbar[...], preferred_element_type=f32)

    for slab in range(1, SLABS):
        forward_sums(slab)
        finish(slab - 1)
    finish(SLABS - 1)

    for slab in range(SLABS):
        swap_copy(slab).wait_recv()
        out_ref[:, columns(1 - core, slab)] = swap_in[slab]

    for slab in range(SLABS):
        grad_copy(slab).wait_send()
        far_copy(slab).wait_send()
        swap_copy(slab).wait_send()

    @pl.loop(0, 4 * SLABS)
    def _(step):
        x_copy(step).wait_send()

    @pl.loop(0, 2 * SLABS)
    def _(step):
        near_copy(step).wait_send()

    for gather in (img, gbars, texts, pooleds):
        gather.wait_sent()
    mp_copy.wait_send()
    t_copy.wait_send()


def whole(tokens, lengths, images, pair_group, w_up, w_down, total):
    count, width = tokens.shape
    captions = images.shape[0]
    hidden = w_up.shape[0]
    slab = slab_width(hidden)
    padded = 2 * SLABS * slab
    rows = width // 8
    own_rows = rows // 2
    bf16, f32 = jnp.bfloat16, jnp.float32
    vmem = pl.BlockSpec(memory_space=pltpu.VMEM)
    hbm = pl.BlockSpec(memory_space=pl.ANY)
    dma = pltpu.SemaphoreType.DMA
    shape = jax.ShapeDtypeStruct
    return pl.pallas_call(
        functools.partial(whole_kernel, total),
        out_shape=(
            shape((1, captions), f32),
            shape((captions, width), f32),
            shape((own_rows, padded), f32),
            shape((own_rows, hidden), f32),
        ),
        in_specs=[vmem] * 4 + [hbm] * 2,
        out_specs=(vmem,) * 4,
        scratch_shapes=[
            pltpu.VMEM((width, total), f32),
            pltpu.VMEM((total, width), bf16),
            pltpu.VMEM((total, hidden), bf16),
            pltpu.VMEM((count, LANES), f32),
            pltpu.VMEM((total, width), bf16),
            pltpu.VMEM((captions, padded), f32),
            pltpu.VMEM((count, padded), f32),
            pltpu.VMEM((width, count), bf16),
            pltpu.VMEM((width, count), bf16),
            pltpu.VMEM(w_up.shape, bf16),
            pltpu.VMEM(w_down.shape, bf16),
            pltpu.VMEM((count, width), bf16),
            pltpu.VMEM((count // 2, slab), f32),
            pltpu.VMEM((count // 2, slab), f32),
            pltpu.VMEM((captions, padded), f32),
            pltpu.VMEM((captions, width), f32),
            pltpu.VMEM((total, width), bf16),
            pltpu.VMEM((captions, width), f32),
            pltpu.VMEM((captions, width), f32),
            pltpu.VMEM((count, padded), bf16),
            pltpu.VMEM((SLABS, count, slab), bf16),
            pltpu.VMEM((4, SLABS, rows, slab), f32),
            pltpu.VMEM((4 * SLABS, rows, slab), bf16),
            pltpu.VMEM((4 * SLABS, rows, slab), bf16),
            pltpu.VMEM((2 * SLABS, rows, slab), bf16),
            pltpu.VMEM((2 * SLABS, rows, slab), bf16),
            pltpu.VMEM((SLABS, rows, slab), bf16),
            pltpu.VMEM((SLABS, rows, slab), bf16),
            pltpu.VMEM((SLABS, own_rows, slab), f32),
            pltpu.VMEM((SLABS, own_rows, slab), f32),
            dma((2,)),
            dma((2, 15)),
            dma((2, 1)),
            dma((2, 1)),
            dma((2, 15)),
            dma((2, 15)),
            dma((2, 15)),
            dma((2, SLABS)),
            dma((2, 4 * SLABS)),
            dma((2, 2 * SLABS)),
            dma((2, SLABS)),
            dma((2, SLABS)),
        ],
        cost_estimate=pl.CostEstimate(
            flops=4 * count * width * hidden, bytes_accessed=4 * width * hidden,
            transcendentals=count * hidden,
        ),
        compiler_params=pltpu.CompilerParams(
            collective_id=0, has_side_effects=True, vmem_limit_bytes=60 * 1024 * 1024
        ),
    )(
        tokens,
        lengths.reshape(1, captions),
        images,
        pair_group.reshape(1, total),
        w_up,
        w_down,
    )


def on_device(tokens, lengths, images, pair_group, w_up, w_down):
    captions = lengths.shape[0]
    seq_len = tokens.shape[0] // captions
    width = tokens.shape[1]
    hidden = w_up.shape[1]
    devices = lax.axis_size("dp")
    own_index = lax.axis_index("dp")
    total = captions * devices
    own_rows = width // devices
    own_group = lax.dynamic_slice_in_dim(pair_group, own_index * captions, captions)
    position = jnp.arange(seq_len, dtype=jnp.int32)
    valid = (position[None, :] < lengths[:, None]).astype(jnp.float32)
    share = valid / jnp.sum(valid, 1, keepdims=True)
    unit_image, image_scale = unit_rows(images.astype(jnp.float32))
    image_half = unit_image.astype(jnp.bfloat16)

    by_chips = devices == 16 and lax.axis_size("mp") == 2 and captions == 16
    if by_chips:
        loss, image_grad, up_grad, down_grad = whole(
            tokens, lengths, images, pair_group, w_up.T, w_down.T, total
        )
        caption_loss = loss.reshape(captions)
        up_grad = up_grad[:, :hidden]
    else:
        all_images = lax.all_gather(image_half, "dp", axis=0, tiled=True)
        tok_float = tokens.astype(jnp.float32)
        normed = layer_norm(tok_float).astype(jnp.bfloat16)
        pre = jnp.dot(normed, w_up, preferred_element_type=jnp.float32)
        value, slope = gelu_pair(pre)
        gmean = jnp.sum(value.reshape(captions, seq_len, hidden) * share[:, :, None], 1)
        tmean = jnp.sum(tok_float.reshape(captions, seq_len, width) * share[:, :, None], 1)
        gbar = gmean.astype(jnp.bfloat16)
        partial_value = lax.dot_general(
            gbar, w_down, (((1,), (1,)), ((), ())), preferred_element_type=jnp.float32
        )
        pooled = tmean + lax.psum(partial_value, "mp")
        unit_text, text_scale = unit_rows(pooled)
        text_half = unit_text.astype(jnp.bfloat16)
        signs, signed = signed_logits(
            text_half, own_group[:, None], all_images, pair_group[None, :]
        )
        caption_loss = -jnp.sum(jax.nn.log_sigmoid(signed), 1) / total
        text_back = jnp.dot(
            loss_slope(signs, signed), all_images, preferred_element_type=jnp.float32
        )
        pooled_half = through_unit(text_back, unit_text, text_scale).astype(jnp.bfloat16)
        hidden_grad = jnp.dot(pooled_half, w_down, preferred_element_type=jnp.float32)
        pre_grad = (
            share[:, :, None] * hidden_grad[:, None, :] * slope.reshape(captions, seq_len, hidden)
        ).astype(jnp.bfloat16)
        pre_grad = pre_grad.reshape(captions * seq_len, hidden)
        up_grad = lax.psum_scatter(
            lax.dot_general(
                normed, pre_grad, (((0,), (0,)), ((), ())), preferred_element_type=jnp.float32
            ),
            "dp",
            scatter_dimension=0,
            tiled=True,
        )
        gathered = lax.all_gather(
            jnp.concatenate([text_half, pooled_half, gbar], 1), "dp", axis=0, tiled=True
        )
        all_texts = gathered[:, :width]
        all_pooled = gathered[:, width : 2 * width]
        all_gbar = gathered[:, 2 * width :]
        unit_image, image_scale = unit_rows(images.astype(jnp.float32))
        image_half = unit_image.astype(jnp.bfloat16)
        signs, signed = signed_logits(
            all_texts, pair_group[:, None], image_half, own_group[None, :]
        )
        image_back = lax.dot_general(
            loss_slope(signs, signed), all_texts, (((0,), (0,)), ((), ())),
            preferred_element_type=jnp.float32,
        )
        image_grad = through_unit(image_back, unit_image, image_scale)
        own_pooled = lax.dynamic_slice_in_dim(all_pooled, own_index * own_rows, own_rows, 1)
        down_grad = lax.dot_general(
            own_pooled, all_gbar, (((0,), (0,)), ((), ())), preferred_element_type=jnp.float32
        )
    return (caption_loss, image_grad, up_grad, down_grad)


def solution(mesh):
    in_specs = (P("dp", None), P("dp"), P("dp", None), P(), P(None, "mp"), P(None, "mp"))
    out_specs = (P("dp"), P("dp", None), P("dp", "mp"), P("dp", "mp"))
    return jax.shard_map(
        on_device, mesh=mesh, in_specs=in_specs, out_specs=out_specs, check_vma=False
    )
```
